32 devices in a mesh: gx: 8 (over y, x, core), gy: 4 (over z).
Axes of the slice: x: 2, y: 2, z: 4, core: 2. Of those that a mesh axis runs over, the one named last changes fastest.
Arguments:
- field: bfloat16 [64, 128, 512], P(None, 'gx', 'gy'), may hold values from -6 to 6
- spectral_weight: bfloat16 [2, 128, 128, 64, 64], P(None, 'gx', 'gy'), may hold values from -1.5 to 1.5
- kernel_weight: bfloat16 [3, 3, 64, 64], replicated, may hold values from -1 to 1
- cotangent: bfloat16 [64, 128, 512], P(None, 'gx', 'gy'), may hold values from -6 to 6
Outputs:
- layer_out: bfloat16 [64, 128, 512], P(None, 'gx', 'gy')
- field_grad: bfloat16 [64, 128, 512], P(None, 'gx', 'gy')
- spectral_grad: bfloat16 [2, 128, 128, 64, 64], P(None, 'gx', 'gy')
- kernel_grad: float32 [3, 3, 64, 64], replicated
The draws below stay inside these ranges and needn't reach their ends.
All inputs are finite; a program needn't handle non-finite values.
Results may differ from the reference program's by a relative error of at most 0.009.
Values may be sent and summed in bfloat16 or wider, within the bound.
No kernel may reach another device: no remote copies, remote signals or barrier semaphores. Data moves between devices by JAX's collectives and lax.ppermute only.
A program may use at most 128 MiB of HBM per device.

```python
import math
from functools import partial
import jax
import jax.numpy as jnp
from jax import lax

C = 64
KX = 128
KY = 128
NX = 128
NY = 512


def levels(stream_key, dims, split, smallest, largest):
    loudness = 1.0
    for position, parts in split:
        heights = jax.random.uniform(jax.random.fold_in(jax.random.fold_in(stream_key, 6), position), (parts,), jnp.float32, smallest / len(split), largest / len(split))
        loudness = loudness * jnp.repeat(jnp.exp(heights), dims[position] // parts).reshape((-1,) + (1,) * (len(dims) - 1 - position))
    return loudness


def scatter_about(own_key, shape, width, most, pieces=(), kind=jnp.bfloat16):
    level = levels(own_key, shape, pieces, -0.22, 0.18) if pieces else 1.0
    values = jax.random.normal(own_key, shape, jnp.float32) * width * level
    return jnp.minimum(jnp.maximum(values, -most), most).astype(kind)


def setup_inputs(seed: int = 0) -> dict:
    key_list = jax.random.split(jax.random.key(seed), 5)
    return {
        "field": scatter_about(key_list[0], (C, NX, NY), 1.0, 6.0, ((1, 8), (2, 4))),
        "spectral_weight": scatter_about(key_list[1], (2, KX, KY, C, C), (C // 4) ** -0.5, 1.5, ((1, 8), (2, 4))),
        "kernel_weight": scatter_about(key_list[2], (3, 3, C, C), (C // 2) ** -0.5, 1.0),
        "cotangent": scatter_about(key_list[3], (C, NX, NY), 1.0, 6.0, ((1, 8), (2, 4))),
    }


def phases(waves, points, length):
    wrapped = jnp.mod(waves[:, None] * points[None, :], length).astype(jnp.float32)
    return wrapped * (2.0 * math.pi / length)

def analyse(field):
    col_angles = phases(jnp.arange(KY, dtype=jnp.int32), jnp.arange(NY, dtype=jnp.int32), NY)
    col_table = jnp.concatenate([jnp.cos(col_angles), -jnp.sin(col_angles)], 0).astype(jnp.bfloat16)
    along_y = jnp.dot(field.reshape(C * NX, NY), col_table.T, preferred_element_type=jnp.float32)
    along_y = along_y.reshape(C, NX, 2, KY).transpose(3, 1, 2, 0)
    row_waves = jnp.arange(KX, dtype=jnp.int32) - KX // 2
    row_angles = phases(row_waves, jnp.arange(NX, dtype=jnp.int32), NX)
    cosines = jnp.cos(row_angles)
    sines = jnp.sin(row_angles)
    real_in = along_y[:, :, 0]
    imag_in = along_y[:, :, 1]
    contract = partial(jnp.einsum, 'jx,lxc->jlc', precision=lax.Precision.HIGHEST)
    real_out = contract(cosines, real_in) + contract(sines, imag_in)
    imag_out = contract(cosines, imag_in) - contract(sines, real_in)
    return jnp.stack([real_out, imag_out], 2) * (1.0 / math.sqrt(NX * NY))

def synthesise(modes):
    row_waves = jnp.arange(KX, dtype=jnp.int32) - KX // 2
    row_angles = phases(row_waves, jnp.arange(NX, dtype=jnp.int32), NX)
    cosines = jnp.cos(row_angles).astype(jnp.bfloat16).astype(jnp.float32)
    sines = jnp.sin(row_angles).astype(jnp.bfloat16).astype(jnp.float32)
    real_in = modes[:, :, 0].astype(jnp.float32)
    imag_in = modes[:, :, 1].astype(jnp.float32)
    contract = partial(jnp.einsum, 'jx,jlc->lxc', precision=lax.Precision.HIGHEST)
    real_out = contract(cosines, real_in) - contract(sines, imag_in)
    imag_out = contract(sines, real_in) + contract(cosines, imag_in)
    along_x = jnp.stack([real_out, imag_out], 2).astype(jnp.bfloat16)
    col_angles = phases(jnp.arange(KY, dtype=jnp.int32), jnp.arange(NY, dtype=jnp.int32), NY)
    col_table = jnp.concatenate([jnp.cos(col_angles), -jnp.sin(col_angles)], 0).astype(jnp.bfloat16)
    flat = along_x.transpose(3, 1, 2, 0).reshape(C * NX, 2 * KY)
    result = jnp.dot(flat, col_table, preferred_element_type=jnp.float32)
    return result.reshape(C, NX, NY) * (1.0 / math.sqrt(NX * NY))

def local_kernel(field, kernel_weight):
    running = jnp.zeros((C, NX * NY), jnp.float32)
    for row_tap in range(3):
        for col_tap in range(3):
            moved = jnp.roll(field, (1 - row_tap, 1 - col_tap), axis=(1, 2)).reshape(C, NX * NY)
            running = running + jnp.dot(kernel_weight[row_tap, col_tap], moved, preferred_element_type=jnp.float32)
    return running.reshape(C, NX, NY)

def kernel_adjoint(grads, kernel_weight):
    running = jnp.zeros((C, NX * NY), jnp.float32)
    for row_tap in range(3):
        for col_tap in range(3):
            moved = jnp.roll(grads, (row_tap - 1, col_tap - 1), axis=(1, 2)).reshape(C, NX * NY)
            running = running + jnp.dot(kernel_weight[row_tap, col_tap].T, moved, preferred_element_type=jnp.float32)
    return running.reshape(C, NX, NY)

def kernel_terms(grads, field):
    flat_grads = grads.reshape(C, NX * NY)
    rows_out = []
    for row_tap in range(3):
        taps = []
        for col_tap in range(3):
            moved = jnp.roll(field, (1 - row_tap, 1 - col_tap), axis=(1, 2)).reshape(C, NX * NY)
            taps.append(jnp.dot(flat_grads, moved.T, preferred_element_type=jnp.float32))
        rows_out.append(jnp.stack(taps, 0))
    return jnp.stack(rows_out, 0)

def reference(field, spectral_weight, kernel_weight, cotangent):
    highest = lax.Precision.HIGHEST
    amodes = analyse(field)
    areal = amodes[:, :, 0]
    aimag = amodes[:, :, 1]
    wreal = spectral_weight[0].astype(jnp.float32)
    wimag = spectral_weight[1].astype(jnp.float32)
    mixing = partial(jnp.einsum, 'jli,jlio->jlo', precision=highest)
    breal = mixing(areal, wreal) - mixing(aimag, wimag)
    bimag = mixing(areal, wimag) + mixing(aimag, wreal)
    weights = jnp.where(jnp.arange(KY) == 0, 1.0, 2.0).astype(jnp.float32)[None, :, None, None]
    bmodes = (jnp.stack([breal, bimag], 2) * weights).astype(jnp.bfloat16)
    hidden = local_kernel(field, kernel_weight) + synthesise(bmodes)
    activated, pullback = jax.vjp(jax.nn.gelu, hidden)
    layer_out = (field.astype(jnp.float32) + activated).astype(jnp.bfloat16)
    grads = pullback(cotangent.astype(jnp.float32))[0].astype(jnp.bfloat16)
    gmodes = analyse(grads) * weights
    greal = gmodes[:, :, 0]
    gimag = gmodes[:, :, 1]
    outer = partial(jnp.einsum, 'jli,jlo->jlio', precision=highest)
    spectral_grad = jnp.stack([outer(areal, greal) + outer(aimag, gimag), outer(areal, gimag) - outer(aimag, greal)], 0).astype(jnp.bfloat16)
    back = partial(jnp.einsum, 'jlio,jlo->jli', precision=highest)
    back_real = back(wreal, greal) + back(wimag, gimag)
    back_imag = back(wreal, gimag) - back(wimag, greal)
    back_modes = jnp.stack([back_real, back_imag], 2).astype(jnp.bfloat16)
    field_grad = (cotangent.astype(jnp.float32) + kernel_adjoint(grads, kernel_weight) + synthesise(back_modes)).astype(jnp.bfloat16)
    kernel_grad = kernel_terms(grads, field)
    return (layer_out, field_grad, spectral_grad, kernel_grad)
```

```python
from functools import partial
import math

import jax
import jax.numpy as jnp
import ml_dtypes
import numpy as np
from jax import lax
from jax.experimental import pallas as pl
from jax.experimental.pallas import tpu as pltpu
from jax.sharding import PartitionSpec as P

KX = 128
KY = 128


def extended(array, sides, width):
    for axis, dim in sides:
        count, length = (lax.axis_size(axis), array.shape[dim])
        up = [(i, (i + 1) % count) for i in range(count)]
        down = [(j, i) for i, j in up]
        last = lax.slice_in_dim(array, length - width, length, axis=dim)
        initial = lax.slice_in_dim(array, 0, width, axis=dim)
        before = lax.ppermute(last, axis, up)
        after = lax.ppermute(initial, axis, down)
        array = jnp.concatenate([before, array, after], axis=dim)
    return array


def phases(waves, points, length):
    wrapped = jnp.mod(waves[:, None] * points[None, :], length).astype(jnp.float32)
    return wrapped * (2.0 * math.pi / length)


def widen(field):
    return extended(field, (("gx", 1), ("gy", 2)), 1)


def general_body(field, spectral_weight, kernel_weight, cotangent):
    highest = lax.Precision.HIGHEST
    channels, block_rows, block_cols = field.shape
    rows_total = block_rows * lax.axis_size("gx")
    cols_total = block_cols * lax.axis_size("gy")
    scale = 1.0 / math.sqrt(rows_total * cols_total)
    row_coord = lax.axis_index("gx") * block_rows + jnp.arange(block_rows, dtype=jnp.int32)
    col_coord = lax.axis_index("gy") * block_cols + jnp.arange(block_cols, dtype=jnp.int32)
    modes_x = KX // lax.axis_size("gx")
    modes_y = KY // lax.axis_size("gy")

    def analyse(source):
        waves = jnp.arange(lax.axis_size("gy") * modes_y, dtype=jnp.int32)
        angles = phases(waves, col_coord, cols_total)
        table = jnp.concatenate([jnp.cos(angles), -jnp.sin(angles)], 0).astype(jnp.bfloat16)
        product = jnp.dot(
            source.reshape(channels * block_rows, block_cols),
            table.T,
            preferred_element_type=jnp.float32,
        )
        product = product.reshape(channels, block_rows, 2, lax.axis_size("gy") * modes_y).transpose(
            3, 1, 2, 0
        )
        col_modes = lax.psum_scatter(
            product.reshape(lax.axis_size("gy") * modes_y, block_rows, 2 * channels),
            "gy",
            scatter_dimension=0,
            tiled=True,
        )
        split_modes = col_modes.reshape(modes_y, block_rows, 2, channels)
        real_in = split_modes[:, :, 0]
        imag_in = split_modes[:, :, 1]
        waves = jnp.arange(lax.axis_size("gx") * modes_x, dtype=jnp.int32) - KX // 2
        angles = phases(waves, row_coord, rows_total)
        cosines = jnp.cos(angles)
        sines = jnp.sin(angles)
        contract = partial(jnp.einsum, "jx,lxc->jlc", precision=highest)
        real_out = contract(cosines, real_in) + contract(sines, imag_in)
        imag_out = contract(cosines, imag_in) - contract(sines, real_in)
        return lax.psum_scatter(
            jnp.stack([real_out, imag_out], 2).reshape(
                lax.axis_size("gx") * modes_x, modes_y, 2 * channels
            )
            * scale,
            "gx",
            scatter_dimension=0,
            tiled=True,
        ).reshape(modes_x, modes_y, 2, channels)

    def synthesise(modes):
        start_rows = jnp.zeros((modes_y, block_rows, 2 * channels), jnp.float32)
        shard_rows = lax.all_gather(
            modes.reshape(modes_x, modes_y, 2 * channels), "gx", axis=0, tiled=True
        )
        amount = shard_rows.shape[0]
        waves = jnp.arange(amount, dtype=jnp.int32) - KX // 2
        angles = phases(waves, row_coord, rows_total)
        cosines = jnp.cos(angles).astype(jnp.bfloat16)
        sines = jnp.sin(angles).astype(jnp.bfloat16)
        split_rows = shard_rows.reshape(amount, modes_y, 2, channels)
        real_in = split_rows[:, :, 0]
        imag_in = split_rows[:, :, 1]
        contract = partial(jnp.einsum, "jx,jlc->lxc", preferred_element_type=jnp.float32)
        real_out = contract(cosines, real_in) - contract(sines, imag_in)
        imag_out = contract(sines, real_in) + contract(cosines, imag_in)
        row_sum = start_rows + jnp.stack([real_out, imag_out], 2).reshape(
            modes_y, block_rows, 2 * channels
        )
        row_sum = row_sum.astype(jnp.bfloat16)
        shard_rows = lax.all_gather(row_sum, "gy", axis=0, tiled=True)
        amount = shard_rows.shape[0]
        waves = jnp.arange(amount, dtype=jnp.int32)
        angles = phases(waves, col_coord, cols_total)
        table = jnp.stack([jnp.cos(angles), -jnp.sin(angles)], 1).astype(jnp.bfloat16)
        split_rows = shard_rows.reshape(amount, block_rows, 2, channels)
        return (
            jnp.einsum("lxpc,lpy->cxy", split_rows, table, preferred_element_type=jnp.float32)
            * scale
        )

    padded_field = widen(field)
    hidden = jnp.zeros((channels, block_rows, block_cols), jnp.float32)
    for row_tap in range(3):
        for col_tap in range(3):
            window = padded_field[:, row_tap : row_tap + block_rows, col_tap : col_tap + block_cols]
            hidden = hidden + jnp.einsum(
                "oi,ixy->oxy",
                kernel_weight[row_tap, col_tap],
                window,
                preferred_element_type=jnp.float32,
            )
    amodes = analyse(field)
    areal = amodes[:, :, 0]
    aimag = amodes[:, :, 1]
    wreal = spectral_weight[0].astype(jnp.float32)
    wimag = spectral_weight[1].astype(jnp.float32)
    mixing = partial(jnp.einsum, "jli,jlio->jlo", precision=highest)
    breal = mixing(areal, wreal) - mixing(aimag, wimag)
    bimag = mixing(areal, wimag) + mixing(aimag, wreal)
    wave_index = lax.axis_index("gy") * modes_y + jnp.arange(modes_y, dtype=jnp.int32)
    weights = jnp.where(wave_index == 0, 1.0, 2.0).astype(jnp.float32)[None, :, None, None]
    bmodes = (jnp.stack([breal, bimag], 2) * weights).astype(jnp.bfloat16)
    hidden = hidden + synthesise(bmodes)
    activated, pullback = jax.vjp(jax.nn.gelu, hidden)
    layer_out = (field.astype(jnp.float32) + activated).astype(jnp.bfloat16)
    grads = pullback(cotangent.astype(jnp.float32))[0].astype(jnp.bfloat16)
    gmodes = analyse(grads) * weights
    greal = gmodes[:, :, 0]
    gimag = gmodes[:, :, 1]
    outer = partial(jnp.einsum, "jli,jlo->jlio", precision=highest)
    spectral_grad = jnp.stack(
        [outer(areal, greal) + outer(aimag, gimag), outer(areal, gimag) - outer(aimag, greal)], 0
    ).astype(jnp.bfloat16)
    back = partial(jnp.einsum, "jlio,jlo->jli", precision=highest)
    back_real = back(wreal, greal) + back(wimag, gimag)
    back_imag = back(wreal, gimag) - back(wimag, greal)
    back_modes = jnp.stack([back_real, back_imag], 2).astype(jnp.bfloat16)
    padded_grads = widen(grads)
    adjoint = jnp.zeros((channels, block_rows, block_cols), jnp.float32)
    tap_rows = []
    for row_tap in range(3):
        tap_cols = []
        for col_tap in range(3):
            window = padded_grads[
                :, 2 - row_tap : 2 - row_tap + block_rows, 2 - col_tap : 2 - col_tap + block_cols
            ]
            adjoint = adjoint + jnp.einsum(
                "oi,oxy->ixy",
                kernel_weight[row_tap, col_tap],
                window,
                preferred_element_type=jnp.float32,
            )
            source_window = padded_field[
                :, row_tap : row_tap + block_rows, col_tap : col_tap + block_cols
            ]
            tap_cols.append(
                jnp.einsum("oxy,ixy->oi", grads, source_window, preferred_element_type=jnp.float32)
            )
        tap_rows.append(jnp.stack(tap_cols, 0))
    kernel_grad = lax.psum(jnp.stack(tap_rows, 0), ("gx", "gy"))
    field_grad = (cotangent.astype(jnp.float32) + adjoint + synthesise(back_modes)).astype(
        jnp.bfloat16
    )
    return (layer_out, field_grad, spectral_grad, kernel_grad)


BF16 = jnp.bfloat16
F32 = jnp.float32
BOTH = ("gx", "gy")
VMEM = 48 * 1024 * 1024


def whole(count):
    return [pl.BlockSpec(memory_space=pltpu.VMEM)] * count


class Plan:
    def __init__(self, channels, block_rows, block_cols, gx, gy):
        self.gx, self.gy, self.devices = gx, gy, gx * gy
        self.channels, self.bx, self.by = channels, block_rows, block_cols
        self.nx, self.ny = block_rows * gx, block_cols * gy
        self.mx, self.my = KX // gx, KY // gy
        self.cpd = channels // self.devices if channels % self.devices == 0 else 0
        self.lanes = self.cpd * 2 * self.my
        self.fits = (
            self.cpd > 0
            and self.lanes == 128
            and KX % gx == 0
            and KY % gy == 0
            and self.bx % 16 == 0
            and self.by % 128 == 0
            and self.mx % 16 == 0
            and self.my % 8 == 0
            and KX % 128 == 0
            and self.nx % 128 == 0
            and self.channels == 64
        )
        self.scale = 1.0 / math.sqrt(self.nx * self.ny)

    def tables(self):
        two_pi = np.float32(2.0 * math.pi)
        waves, points = np.arange(KY), np.arange(self.ny)
        angles = np.float32((waves[:, None] * points[None, :]) % self.ny) * (two_pi / self.ny)
        cos, sin = np.cos(angles).T, np.sin(angles).T
        col = np.zeros((self.cpd, self.ny, 2, self.gy, self.cpd, 2, self.my), np.float32)
        for c in range(self.cpd):
            split = (self.ny, self.gy, self.my)
            col[c, :, 0, :, c, 0] = cos.reshape(split)
            col[c, :, 0, :, c, 1] = -sin.reshape(split)
            col[c, :, 1, :, c, 0] = -sin.reshape(split)
            col[c, :, 1, :, c, 1] = -cos.reshape(split)
        col = col.reshape(self.cpd * self.ny, -1).astype(ml_dtypes.bfloat16)
        rows = np.arange(KX) - KX // 2
        points = np.arange(self.nx)
        angles = np.float32((rows[:, None] * points[None, :]) % self.nx) * (two_pi / self.nx)
        row = np.concatenate([np.cos(angles), np.sin(angles)], 1).astype(np.float32)
        high = row.astype(ml_dtypes.bfloat16)
        low = (row - high.astype(np.float32)).astype(ml_dtypes.bfloat16)
        row_analysis = np.concatenate([high, low], 1)
        row_synthesis = np.concatenate([np.cos(angles).T, np.sin(angles).T], 0)
        row_synthesis = row_synthesis.astype(ml_dtypes.bfloat16)
        doubled = np.full((self.gy, self.cpd, 2, self.my), 2.0, np.float32)
        doubled[0, :, :, 0] = 1.0
        doubled = doubled.reshape(1, -1)
        return col, np.ascontiguousarray(col.T), row_analysis, row_synthesis, doubled


def dot(a, b):
    return jnp.dot(a, b, preferred_element_type=F32)


def analyse_plane(plan, planes, col, row, weight, out_ref):
    half = col.shape[1] // 2
    along_y = dot(planes, col[...]).astype(BF16)
    stacked = jnp.concatenate([along_y[:, :half], along_y[:, half:]], 0)
    modes = dot(row[...], jnp.concatenate([stacked, stacked], 0)) * weight
    modes = modes.astype(BF16)
    for i in range(plan.gx):
        for k in range(plan.gy):
            out_ref[i * plan.gy + k] = modes[
                i * plan.mx : (i + 1) * plan.mx, k * plan.lanes : (k + 1) * plan.lanes
            ]


def synthesise_plane(plan, modes_ref, row, col_t, weight):
    columns = []
    for k in range(plan.gy):
        columns.append(jnp.concatenate([modes_ref[i * plan.gy + k] for i in range(plan.gx)], 0))
    sums = dot(row[...], jnp.concatenate(columns, 1))
    if weight is not None:
        sums = sums * weight
    sums = sums.astype(BF16)
    return dot(jnp.concatenate([sums[: plan.nx], sums[plan.nx :]], 1), col_t[...])


def read_plane(plan, ref, c, k):
    return jnp.concatenate([ref[i * plan.gy + k, c] for i in range(plan.gx)], 0)


def write_planes(plan, ref, planes):
    for c in range(plan.cpd):
        for k in range(plan.gy):
            start = c * plan.ny + k * plan.by
            for i in range(plan.gx):
                ref[i * plan.gy + k, c] = planes[
                    i * plan.bx : (i + 1) * plan.bx, start : start + plan.by
                ]


def first_kernel(plan, field_ref, col, row, out_ref):
    planes = [read_plane(plan, field_ref, c, k) for c in range(plan.cpd) for k in range(plan.gy)]
    analyse_plane(plan, jnp.concatenate(planes, 1), col, row, plan.scale, out_ref)


def gelu_parts(z):
    cubic = math.sqrt(2.0 / math.pi)
    inner = cubic * (z + 0.044715 * (z * z * z))
    tanh = jnp.tanh(inner)
    cdf = 0.5 * (1.0 + tanh)
    slope = cdf + 0.5 * z * (1.0 - tanh * tanh) * (cubic * (1.0 + (3.0 * 0.044715) * (z * z)))
    return z * cdf, slope


def middle_kernel(
    plan, modes_ref, conv_ref, cot_ref, col, col_t, row, row_s, doubled, out_ref, z_ref, grads
):
    syn = synthesise_plane(plan, modes_ref, row_s, col_t, doubled[...]) * plan.scale
    for c in range(plan.cpd):
        for k in range(plan.gy):
            start = c * plan.ny + k * plan.by
            z = syn[:, start : start + plan.by] + read_plane(plan, conv_ref, c, k).astype(F32)
            z = z.astype(BF16)
            for i in range(plan.gx):
                z_ref[i * plan.gy + k, c] = z[i * plan.bx : (i + 1) * plan.bx]
            slope = gelu_parts(z.astype(F32))[1]
            cot = read_plane(plan, cot_ref, c, k).astype(F32)
            grads[:, start : start + plan.by] = (cot * slope).astype(BF16)
    analyse_plane(plan, grads[...], col, row, doubled[...] * plan.scale, out_ref)


def last_kernel(plan, modes_ref, col_t, row_s, syn_ref):
    syn = synthesise_plane(plan, modes_ref, row_s, col_t, None) * plan.scale
    write_planes(plan, syn_ref, syn.astype(BF16))


def group_mask(rows, groups, width):
    row = lax.broadcasted_iota(jnp.int32, (rows, groups * width), 0)
    lane = lax.broadcasted_iota(jnp.int32, (rows, groups * width), 1)
    return lax.rem(row, groups) == lax.div(lane, width)


def modes_to_rows(plan, x_ref, scratch):
    half = plan.lanes // 2
    values = x_ref[...].astype(F32)
    for j in range(plan.mx):
        turned = values[:, j, :].T
        scratch[j] = jnp.concatenate([turned[:half], turned[half:]], 1)


def rows_to_modes(plan, y_scratch, y_ref):
    y_ref[...] = jnp.swapaxes(y_scratch[...], 0, 1).astype(BF16)


def put_rows(plan, rows, y_scratch, j):
    turned = rows.T
    s = plan.devices
    y_scratch[j] = jnp.concatenate([turned[i * s : (i + 1) * s] for i in range(plan.cpd)], 1)


def mix_kernel(plan, x_ref, r_ref, y_ref, rows, y_scratch):
    j = pl.program_id(0)

    @pl.when(j == 0)
    def _():
        modes_to_rows(plan, x_ref, rows)

    group, width = 8, plan.channels
    mask = group_mask(2 * group, group, width)
    real_out, imag_out = [], []
    for g in range(plan.my // group):
        real = rows[j, g * group : (g + 1) * group, :]
        imag = rows[j, plan.my + g * group : plan.my + (g + 1) * group, :]
        first = jnp.concatenate([jnp.concatenate([real, imag], 0)] * group, 1)
        second = jnp.concatenate([jnp.concatenate([-imag, real], 0)] * group, 1)
        first = jnp.where(mask, first, 0.0).astype(BF16)
        second = jnp.where(mask, second, 0.0).astype(BF16)
        r_real = r_ref[0, 0, g * group : (g + 1) * group].reshape(group * width, width)
        r_imag = r_ref[1, 0, g * group : (g + 1) * group].reshape(group * width, width)
        mixed = dot(first, r_real) + dot(second, r_imag)
        real_out.append(mixed[:group])
        imag_out.append(mixed[group:])
    put_rows(plan, jnp.concatenate(real_out + imag_out, 0), y_scratch, j)

    @pl.when(j == plan.mx - 1)
    def _():
        rows_to_modes(plan, y_scratch, y_ref)


def dot_nt(a, b):
    return lax.dot_general(a, b, (((1,), (1,)), ((), ())), preferred_element_type=F32)


def back_kernel(plan, g_ref, r_ref, y_ref, rows, y_scratch):
    j = pl.program_id(0)

    @pl.when(j == 0)
    def _():
        modes_to_rows(plan, g_ref, rows)

    group, width = 8, plan.channels
    mask = group_mask(2 * group, group, width)
    real_out, imag_out = [], []
    for g in range(plan.my // group):
        real = rows[j, g * group : (g + 1) * group, :]
        imag = rows[j, plan.my + g * group : plan.my + (g + 1) * group, :]
        first = jnp.concatenate([real, imag], 0).astype(BF16)
        second = jnp.concatenate([imag, -real], 0).astype(BF16)
        r_real = r_ref[0, 0, g * group : (g + 1) * group].reshape(group * width, width)
        r_imag = r_ref[1, 0, g * group : (g + 1) * group].reshape(group * width, width)
        mixed = dot_nt(first, r_real) + dot_nt(second, r_imag)
        mixed = jnp.where(mask, mixed, 0.0)
        total = mixed[:, :width]
        for i in range(1, group):
            total = total + mixed[:, i * width : (i + 1) * width]
        real_out.append(total[:group])
        imag_out.append(total[group:])
    put_rows(plan, jnp.concatenate(real_out + imag_out, 0), y_scratch, j)

    @pl.when(j == plan.mx - 1)
    def _():
        rows_to_modes(plan, y_scratch, y_ref)


def outer_kernel(plan, x_ref, g_ref, out_ref, a_rows, g_rows):
    j = pl.program_id(0)

    @pl.when(j == 0)
    def _():
        modes_to_rows(plan, x_ref, a_rows)
        modes_to_rows(plan, g_ref, g_rows)

    my, width = plan.my, plan.channels
    a_turned = a_rows[j].T
    g_real, g_imag = g_rows[j, :my, :], g_rows[j, my:, :]
    first = jnp.concatenate([g_real, g_imag], 0).astype(BF16)
    second = jnp.concatenate([g_imag, -g_real], 0).astype(BF16)
    lane = lax.rem(lax.broadcasted_iota(jnp.int32, (width, 2 * my), 1), my)
    group = 8
    for g in range(my // group):
        left = jnp.concatenate(
            [jnp.where(lane == g * group + l, a_turned, 0.0) for l in range(group)], 0
        ).astype(BF16)
        for part, right in ((0, first), (1, second)):
            value = dot(left, right).astype(BF16)
            out_ref[part, 0, g * group : (g + 1) * group] = value.reshape(group, width, width)


def shift_kernel(plan, block_ref, rows_ref, cols_ref, weights_ref, after_ref, out_ref, taps_ref):
    c, by, bx = plan.channels, plan.by, plan.bx
    lane = lax.broadcasted_iota(jnp.int32, (c, by), 1)
    for x in range(bx + 2):
        if x == 0:
            row = rows_ref[0]
        elif x == bx + 1:
            row = rows_ref[1]
        else:
            row = block_ref[:, (x - 1) * by : x * by]
        lanes = slice(x * by, (x + 1) * by)
        wide = row.astype(F32)
        left = cols_ref[0, :, x : x + 1].astype(F32)
        right = cols_ref[1, :, x : x + 1].astype(F32)
        taps_ref[:c, lanes] = jnp.where(lane == 0, left, pltpu.roll(wide, 1, 1)).astype(BF16)
        taps_ref[c : 2 * c, lanes] = row
        taps_ref[2 * c :, lanes] = jnp.where(
            lane == by - 1, right, pltpu.roll(wide, by - 1, 1)
        ).astype(BF16)
    for a in range(3):
        part = dot(weights_ref[a], taps_ref[:, a * by : (a + bx) * by])
        if a == 0:
            total = part
        else:
            total = total + part
    out_ref[...] = total.astype(out_ref.dtype)


def taps_kernel(plan, grads_ref, taps_ref, out_ref):
    for a in range(3):
        out_ref[a] = dot_nt(grads_ref[...], taps_ref[:, a * plan.by : (a + plan.bx) * plan.by])


def halo(block):
    def swap(low, high, axis):
        count = lax.axis_size(axis)
        up = [(i, (i + 1) % count) for i in range(count)]
        down = [(j, i) for i, j in up]
        return lax.ppermute(high, axis, up), lax.ppermute(low, axis, down)

    top, bottom = swap(block[:, 0, :], block[:, -1, :], "gx")

    def column(y):
        return jnp.concatenate([top[:, y, None], block[:, :, y], bottom[:, y, None]], 1)

    left, right = swap(column(0), column(-1), "gy")
    return jnp.stack([top, bottom], 0), jnp.stack([left, right], 0)


def fast_body(plan, field, spectral_weight, kernel_weight, cotangent):
    channels, bx, by, n, cpd = plan.channels, plan.bx, plan.by, plan.devices, plan.cpd
    col, col_t, row, row_s, doubled = (jnp.asarray(t) for t in plan.tables())
    params = pltpu.CompilerParams(vmem_limit_bytes=VMEM)
    mode_shape = jax.ShapeDtypeStruct((n, plan.mx, plan.lanes), BF16)
    block_shape = jax.ShapeDtypeStruct((n, cpd, bx, by), BF16)
    taps_shape = jax.ShapeDtypeStruct((3 * channels, (bx + 2) * by), BF16)
    anywhere = pl.BlockSpec(memory_space=pl.ANY)

    def exchange(x):
        return lax.all_to_all(x, BOTH, 0, 0, tiled=True)

    def to_channels(x):
        return exchange(x.reshape(cpd, n, bx, by).transpose(1, 0, 2, 3))

    def to_space(x):
        return x.transpose(1, 0, 2, 3).reshape(channels, bx, by)

    def call(kernel, out_shape, *args, scratch=(), last=None):
        several = isinstance(out_shape, tuple)
        specs = whole(len(args))
        if last is not None:
            specs, args = specs + [anywhere], args + (last,)
        return pl.pallas_call(
            partial(kernel, plan),
            out_shape=out_shape,
            in_specs=specs,
            out_specs=tuple(whole(len(out_shape))) if several else whole(1)[0],
            scratch_shapes=scratch,
            compiler_params=params,
        )(*args)

    weight_spec = pl.BlockSpec(
        (2, 1, plan.my, channels, channels), lambda j: (0, j, 0, 0, 0)
    )
    mode_spec = pl.BlockSpec((n, plan.mx, plan.lanes), lambda j: (0, 0, 0))
    rows_scratch = pltpu.VMEM((plan.mx, 2 * plan.my, channels), F32)
    y_scratch = pltpu.VMEM((plan.mx, n, plan.lanes), F32)

    def mode_call(kernel, x):
        return pl.pallas_call(
            partial(kernel, plan),
            grid=(plan.mx,),
            out_shape=mode_shape,
            in_specs=[mode_spec, weight_spec],
            out_specs=mode_spec,
            scratch_shapes=[rows_scratch, y_scratch],
            compiler_params=params,
        )(x, spectral_weight)

    forward_weight = kernel_weight.transpose(0, 2, 1, 3).reshape(3, channels, 3 * channels)
    adjoint_weight = kernel_weight[::-1, ::-1].transpose(0, 3, 1, 2)
    adjoint_weight = adjoint_weight.reshape(3, channels, 3 * channels)

    field_c = to_channels(field)
    a_part = call(first_kernel, mode_shape, field_c, col, row)
    a_modes = exchange(a_part)
    edge_rows, edge_cols = halo(field)
    conv, taps = call(
        shift_kernel,
        (jax.ShapeDtypeStruct((channels, bx * by), BF16), taps_shape),
        field.reshape(channels, bx * by),
        edge_rows,
        edge_cols,
        forward_weight,
        last=a_part,
    )
    cotangent_late, _ = lax.optimization_barrier((cotangent, a_part))
    cot_c = to_channels(cotangent_late)
    conv_c = to_channels(conv)

    b_modes = exchange(mode_call(mix_kernel, a_modes))
    g_part, z_part = call(
        middle_kernel,
        (mode_shape, block_shape),
        b_modes,
        conv_c,
        cot_c,
        col,
        col_t,
        row,
        row_s,
        doubled,
        scratch=[pltpu.VMEM((plan.nx, cpd * plan.ny), BF16)],
    )
    g_modes = exchange(g_part)
    hidden = to_space(exchange(z_part)).astype(F32)
    activated, slope = gelu_parts(hidden)
    layer_out = (field.astype(F32) + activated).astype(BF16)
    grads = (cotangent.astype(F32) * slope).astype(BF16)
    grads_flat = grads.reshape(channels, bx * by)
    kernel_terms = call(
        taps_kernel, jax.ShapeDtypeStruct((3, channels, 3 * channels), F32), grads_flat, taps
    )
    back_part = mode_call(back_kernel, g_modes)
    piece = 9 * channels * channels // (n * 128)
    terms = kernel_terms.reshape(n, piece, 128).astype(BF16)
    terms = jnp.pad(terms, ((0, 0), (0, -piece % 16), (0, 0)))
    back_both = exchange(jnp.concatenate([back_part, terms], 1))
    back_modes = back_both[:, : plan.mx]
    summed = back_both[:, plan.mx :].astype(F32).sum(0).astype(BF16)
    synthesis_part = call(last_kernel, block_shape, back_modes, col_t, row_s)
    last_part = jnp.concatenate(
        [
            synthesis_part.reshape(n, cpd * bx, by),
            jnp.broadcast_to(summed[None], (n,) + summed.shape),
        ],
        1,
    )
    last_both = exchange(last_part)
    synthesis = to_space(last_both[:, : cpd * bx].reshape(n, cpd, bx, by))
    kernel_grad = last_both[:, cpd * bx : cpd * bx + piece].astype(F32)
    kernel_grad = kernel_grad.reshape(3, channels, 3, channels).transpose(0, 2, 1, 3)

    spectral_grad = pl.pallas_call(
        lambda x, g, after, *rest: outer_kernel(plan, x, g, *rest),
        grid=(plan.mx,),
        out_shape=jax.ShapeDtypeStruct(spectral_weight.shape, BF16),
        in_specs=[mode_spec, mode_spec, anywhere],
        out_specs=weight_spec,
        scratch_shapes=[rows_scratch, rows_scratch],
        compiler_params=params,
    )(a_modes, g_modes, back_part)

    grad_rows, grad_cols = halo(grads)
    adjoint, _ = call(
        shift_kernel,
        (jax.ShapeDtypeStruct((channels, bx * by), F32), taps_shape),
        grads_flat,
        grad_rows,
        grad_cols,
        adjoint_weight,
        last=back_part,
    )
    field_grad = cotangent.astype(F32) + adjoint.reshape(channels, bx, by) + synthesis.astype(F32)
    return (layer_out, field_grad.astype(BF16), spectral_grad, kernel_grad)


def body(field, spectral_weight, kernel_weight, cotangent):
    plan = Plan(*field.shape, lax.axis_size("gx"), lax.axis_size("gy"))
    if plan.fits:
        return fast_body(plan, field, spectral_weight, kernel_weight, cotangent)
    return general_body(field, spectral_weight, kernel_weight, cotangent)


def solution(mesh):
    in_specs = (P(None, "gx", "gy"), P(None, "gx", "gy", None, None), P(), P(None, "gx", "gy"))
    out_specs = (P(None, "gx", "gy"), P(None, "gx", "gy"), P(None, "gx", "gy", None, None), P())
    return jax.shard_map(body, mesh=mesh, in_specs=in_specs, out_specs=out_specs, check_vma=False)
```

```python
from functools import partial
import math

import jax
import jax.numpy as jnp
import ml_dtypes
import numpy as np
from jax import lax
from jax.experimental import pallas as pl
from jax.experimental.pallas import tpu as pltpu
from jax.sharding import PartitionSpec as P

KX = 128
KY = 128


def extended(array, sides, width):
    for axis, dim in sides:
        count, length = (lax.axis_size(axis), array.shape[dim])
        up = [(i, (i + 1) % count) for i in range(count)]
        down = [(j, i) for i, j in up]
        last = lax.slice_in_dim(array, length - width, length, axis=dim)
        initial = lax.slice_in_dim(array, 0, width, axis=dim)
        before = lax.ppermute(last, axis, up)
        after = lax.ppermute(initial, axis, down)
        array = jnp.concatenate([before, array, after], axis=dim)
    return array


def phases(waves, points, length):
    wrapped = jnp.mod(waves[:, None] * points[None, :], length).astype(jnp.float32)
    return wrapped * (2.0 * math.pi / length)


def widen(field):
    return extended(field, (("gx", 1), ("gy", 2)), 1)


def general_body(field, spectral_weight, kernel_weight, cotangent):
    highest = lax.Precision.HIGHEST
    channels, block_rows, block_cols = field.shape
    rows_total = block_rows * lax.axis_size("gx")
    cols_total = block_cols * lax.axis_size("gy")
    scale = 1.0 / math.sqrt(rows_total * cols_total)
    row_coord = lax.axis_index("gx") * block_rows + jnp.arange(block_rows, dtype=jnp.int32)
    col_coord = lax.axis_index("gy") * block_cols + jnp.arange(block_cols, dtype=jnp.int32)
    modes_x = KX // lax.axis_size("gx")
    modes_y = KY // lax.axis_size("gy")

    def analyse(source):
        waves = jnp.arange(lax.axis_size("gy") * modes_y, dtype=jnp.int32)
        angles = phases(waves, col_coord, cols_total)
        table = jnp.concatenate([jnp.cos(angles), -jnp.sin(angles)], 0).astype(jnp.bfloat16)
        product = jnp.dot(
            source.reshape(channels * block_rows, block_cols),
            table.T,
            preferred_element_type=jnp.float32,
        )
        product = product.reshape(channels, block_rows, 2, lax.axis_size("gy") * modes_y).transpose(
            3, 1, 2, 0
        )
        col_modes = lax.psum_scatter(
            product.reshape(lax.axis_size("gy") * modes_y, block_rows, 2 * channels),
            "gy",
            scatter_dimension=0,
            tiled=True,
        )
        split_modes = col_modes.reshape(modes_y, block_rows, 2, channels)
        real_in = split_modes[:, :, 0]
        imag_in = split_modes[:, :, 1]
        waves = jnp.arange(lax.axis_size("gx") * modes_x, dtype=jnp.int32) - KX // 2
        angles = phases(waves, row_coord, rows_total)
        cosines = jnp.cos(angles)
        sines = jnp.sin(angles)
        contract = partial(jnp.einsum, "jx,lxc->jlc", precision=highest)
        real_out = contract(cosines, real_in) + contract(sines, imag_in)
        imag_out = contract(cosines, imag_in) - contract(sines, real_in)
        return lax.psum_scatter(
            jnp.stack([real_out, imag_out], 2).reshape(
                lax.axis_size("gx") * modes_x, modes_y, 2 * channels
            )
            * scale,
            "gx",
            scatter_dimension=0,
            tiled=True,
        ).reshape(modes_x, modes_y, 2, channels)

    def synthesise(modes):
        start_rows = jnp.zeros((modes_y, block_rows, 2 * channels), jnp.float32)
        shard_rows = lax.all_gather(
            modes.reshape(modes_x, modes_y, 2 * channels), "gx", axis=0, tiled=True
        )
        amount = shard_rows.shape[0]
        waves = jnp.arange(amount, dtype=jnp.int32) - KX // 2
        angles = phases(waves, row_coord, rows_total)
        cosines = jnp.cos(angles).astype(jnp.bfloat16)
        sines = jnp.sin(angles).astype(jnp.bfloat16)
        split_rows = shard_rows.reshape(amount, modes_y, 2, channels)
        real_in = split_rows[:, :, 0]
        imag_in = split_rows[:, :, 1]
        contract = partial(jnp.einsum, "jx,jlc->lxc", preferred_element_type=jnp.float32)
        real_out = contract(cosines, real_in) - contract(sines, imag_in)
        imag_out = contract(sines, real_in) + contract(cosines, imag_in)
        row_sum = start_rows + jnp.stack([real_out, imag_out], 2).reshape(
            modes_y, block_rows, 2 * channels
        )
        row_sum = row_sum.astype(jnp.bfloat16)
        shard_rows = lax.all_gather(row_sum, "gy", axis=0, tiled=True)
        amount = shard_rows.shape[0]
        waves = jnp.arange(amount, dtype=jnp.int32)
        angles = phases(waves, col_coord, cols_total)
        table = jnp.stack([jnp.cos(angles), -jnp.sin(angles)], 1).astype(jnp.bfloat16)
        split_rows = shard_rows.reshape(amount, block_rows, 2, channels)
        return (
            jnp.einsum("lxpc,lpy->cxy", split_rows, table, preferred_element_type=jnp.float32)
            * scale
        )

    padded_field = widen(field)
    hidden = jnp.zeros((channels, block_rows, block_cols), jnp.float32)
    for row_tap in range(3):
        for col_tap in range(3):
            window = padded_field[:, row_tap : row_tap + block_rows, col_tap : col_tap + block_cols]
            hidden = hidden + jnp.einsum(
                "oi,ixy->oxy",
                kernel_weight[row_tap, col_tap],
                window,
                preferred_element_type=jnp.float32,
            )
    amodes = analyse(field)
    areal = amodes[:, :, 0]
    aimag = amodes[:, :, 1]
    wreal = spectral_weight[0].astype(jnp.float32)
    wimag = spectral_weight[1].astype(jnp.float32)
    mixing = partial(jnp.einsum, "jli,jlio->jlo", precision=highest)
    breal = mixing(areal, wreal) - mixing(aimag, wimag)
    bimag = mixing(areal, wimag) + mixing(aimag, wreal)
    wave_index = lax.axis_index("gy") * modes_y + jnp.arange(modes_y, dtype=jnp.int32)
    weights = jnp.where(wave_index == 0, 1.0, 2.0).astype(jnp.float32)[None, :, None, None]
    bmodes = (jnp.stack([breal, bimag], 2) * weights).astype(jnp.bfloat16)
    hidden = hidden + synthesise(bmodes)
    activated, pullback = jax.vjp(jax.nn.gelu, hidden)
    layer_out = (field.astype(jnp.float32) + activated).astype(jnp.bfloat16)
    grads = pullback(cotangent.astype(jnp.float32))[0].astype(jnp.bfloat16)
    gmodes = analyse(grads) * weights
    greal = gmodes[:, :, 0]
    gimag = gmodes[:, :, 1]
    outer = partial(jnp.einsum, "jli,jlo->jlio", precision=highest)
    spectral_grad = jnp.stack(
        [outer(areal, greal) + outer(aimag, gimag), outer(areal, gimag) - outer(aimag, greal)], 0
    ).astype(jnp.bfloat16)
    back = partial(jnp.einsum, "jlio,jlo->jli", precision=highest)
    back_real = back(wreal, greal) + back(wimag, gimag)
    back_imag = back(wreal, gimag) - back(wimag, greal)
    back_modes = jnp.stack([back_real, back_imag], 2).astype(jnp.bfloat16)
    padded_grads = widen(grads)
    adjoint = jnp.zeros((channels, block_rows, block_cols), jnp.float32)
    tap_rows = []
    for row_tap in range(3):
        tap_cols = []
        for col_tap in range(3):
            window = padded_grads[
                :, 2 - row_tap : 2 - row_tap + block_rows, 2 - col_tap : 2 - col_tap + block_cols
            ]
            adjoint = adjoint + jnp.einsum(
                "oi,oxy->ixy",
                kernel_weight[row_tap, col_tap],
                window,
                preferred_element_type=jnp.float32,
            )
            source_window = padded_field[
                :, row_tap : row_tap + block_rows, col_tap : col_tap + block_cols
            ]
            tap_cols.append(
                jnp.einsum("oxy,ixy->oi", grads, source_window, preferred_element_type=jnp.float32)
            )
        tap_rows.append(jnp.stack(tap_cols, 0))
    kernel_grad = lax.psum(jnp.stack(tap_rows, 0), ("gx", "gy"))
    field_grad = (cotangent.astype(jnp.float32) + adjoint + synthesise(back_modes)).astype(
        jnp.bfloat16
    )
    return (layer_out, field_grad, spectral_grad, kernel_grad)


BF16 = jnp.bfloat16
F32 = jnp.float32
BOTH = ("gx", "gy")
EDGE = 16
GROUP = 8
CHUNK = 2


class Plan:
    def __init__(self, channels, block_rows, block_cols, gx, gy):
        self.gx, self.gy, self.devices = gx, gy, gx * gy
        self.channels, self.bx, self.by = channels, block_rows, block_cols
        self.nx, self.ny = block_rows * gx, block_cols * gy
        self.mx, self.my = KX // gx, KY // gy
        self.cpd = channels // self.devices if channels % self.devices == 0 else 0
        self.lanes = self.cpd * 2 * self.my
        self.rows = self.cpd * self.bx
        self.fits = (
            self.cpd == 2
            and channels == 64
            and self.lanes == 128
            and self.by == 128
            and self.bx == 16
            and KX % gx == 0
            and KY % gy == 0
            and self.mx == 16
            and self.my % GROUP == 0
            and gy % 2 == 0
            and KX == 128
            and self.nx == 128
        )
        self.scale = 1.0 / math.sqrt(self.nx * self.ny)

    def tables(self):
        two_pi = np.float32(2.0 * math.pi)
        waves, points = np.arange(KY), np.arange(self.ny)
        angles = np.float32((waves[:, None] * points[None, :]) % self.ny) * (two_pi / self.ny)
        cos, sin = np.cos(angles).T, np.sin(angles).T
        split = (self.ny, self.gy, self.my)
        cos, sin = cos.reshape(split), sin.reshape(split)
        top, bottom = np.stack([cos, -sin], 2), np.stack([-sin, -cos], 2)
        col = np.stack([top, bottom], 1).reshape(self.ny, -1).astype(ml_dtypes.bfloat16)
        rows = np.arange(KX) - KX // 2
        points = np.arange(self.nx)
        angles = np.float32((rows[:, None] * points[None, :]) % self.nx) * (two_pi / self.nx)
        row = np.concatenate([np.cos(angles), np.sin(angles)], 1).astype(np.float32)
        high = row.astype(ml_dtypes.bfloat16)
        low = (row - high.astype(np.float32)).astype(ml_dtypes.bfloat16)
        row_analysis = np.concatenate([high, low], 1)
        row_synthesis = np.concatenate([np.cos(angles).T, np.sin(angles).T], 0)
        row_synthesis = row_synthesis.astype(ml_dtypes.bfloat16)
        return col, row_analysis, row_synthesis

    def named(self):
        names = ("col", "row", "row_s", "pick_rows", "pick_cols", "window")
        return dict(zip(names, self.tables() + self.pickers()))

    def pickers(self):
        pick_rows = np.zeros((self.gx, EDGE, self.cpd, self.nx), np.float32)
        pick_cols = np.zeros((self.gy, EDGE, self.cpd, self.ny), np.float32)
        window = np.zeros((self.nx, self.gx, self.by), np.float32)
        for c in range(self.cpd):
            for g in range(self.gx):
                pick_rows[g, 2 * c, c, (g * self.bx - 1) % self.nx] = 1
                pick_rows[g, 2 * c + 1, c, ((g + 1) * self.bx) % self.nx] = 1
            for g in range(self.gy):
                pick_cols[g, 2 * self.cpd + 2 * c, c, (g * self.by - 1) % self.ny] = 1
                pick_cols[g, 2 * self.cpd + 2 * c + 1, c, ((g + 1) * self.by) % self.ny] = 1
        for g in range(self.gx):
            for t in range(self.bx + 2):
                window[(g * self.bx - 1 + t) % self.nx, g, t] = 1
        kind = ml_dtypes.bfloat16
        return (
            pick_rows.reshape(self.gx * EDGE, -1).astype(kind),
            pick_cols.reshape(self.gy * EDGE, -1).astype(kind),
            window.reshape(self.nx, -1).astype(kind),
        )


def dot(a, b):
    return jnp.dot(a, b, preferred_element_type=F32)


def dot_nt(a, b):
    return lax.dot_general(a, b, (((1,), (1,)), ((), ())), preferred_element_type=F32)


def interleave(plan, parts):
    half = plan.lanes // 2
    lane = lax.broadcasted_iota(jnp.int32, (1, plan.lanes), 1)
    tiles = []
    for k in range(plan.gy // 2):
        first, second = (p[:, k * plan.lanes : (k + 1) * plan.lanes] for p in parts)
        tiles.append(jnp.where(lane < half, first, pltpu.roll(second, half, 1)))
        tiles.append(jnp.where(lane < half, pltpu.roll(first, half, 1), second))
    return jnp.concatenate(tiles, 1)


def separate(plan, values):
    half = plan.lanes // 2
    lane = lax.broadcasted_iota(jnp.int32, (1, plan.lanes), 1)
    parts = ([], [])
    for k in range(plan.gy // 2):
        even = values[:, 2 * k * plan.lanes : (2 * k + 1) * plan.lanes]
        odd = values[:, (2 * k + 1) * plan.lanes : (2 * k + 2) * plan.lanes]
        parts[0].append(jnp.where(lane < half, even, pltpu.roll(odd, half, 1)))
        parts[1].append(jnp.where(lane < half, pltpu.roll(even, half, 1), odd))
    return [jnp.concatenate(p, 1) for p in parts]


def analyse_plane(plan, held, planes, weight, out_ref):
    col = held["col"]
    half = col.shape[1] // 2
    along_y = [
        dot(planes[:, c * plan.ny : (c + 1) * plan.ny], col[...]) for c in range(plan.cpd)
    ]
    stacked = jnp.concatenate(
        [
            interleave(plan, [p[:, :half] for p in along_y]),
            interleave(plan, [p[:, half:] for p in along_y]),
        ],
        0,
    ).astype(BF16)
    modes = dot(held["row"][...], jnp.concatenate([stacked, stacked], 0)) * weight
    modes = modes.astype(BF16)
    for i in range(plan.gx):
        for k in range(plan.gy):
            out_ref[i * plan.gy + k, : plan.mx] = modes[
                i * plan.mx : (i + 1) * plan.mx, k * plan.lanes : (k + 1) * plan.lanes
            ]


def put_edges(plan, held, planes, out_ref, start):
    stacked = jnp.concatenate(
        [planes[:, c * plan.ny : (c + 1) * plan.ny] for c in range(plan.cpd)], 0
    )
    edge_rows = dot(held["pick_rows"][...], stacked)
    picked = dot_nt(held["pick_cols"][...], planes).astype(BF16)
    edge_cols = dot(picked, held["window"][...])
    for i in range(plan.gx):
        for k in range(plan.gy):
            tile = (
                edge_rows[i * EDGE : (i + 1) * EDGE, k * plan.by : (k + 1) * plan.by]
                + edge_cols[k * EDGE : (k + 1) * EDGE, i * plan.by : (i + 1) * plan.by]
            )
            out_ref[i * plan.gy + k, start : start + EDGE] = tile.astype(BF16)


def synthesise_plane(plan, held, modes_ref, weight):
    columns = []
    for k in range(plan.gy):
        columns.append(
            jnp.concatenate([modes_ref[i * plan.gy + k, : plan.mx] for i in range(plan.gx)], 0)
        )
    sums = dot(held["row_s"][...], jnp.concatenate(columns, 1))
    if weight is not None:
        sums = sums * weight
    top, bottom = separate(plan, sums[: plan.nx]), separate(plan, sums[plan.nx :])
    planes = []
    for c in range(plan.cpd):
        left = jnp.concatenate([top[c], bottom[c]], 1).astype(BF16)
        planes.append(dot_nt(left, held["col"][...]))
    return jnp.concatenate(planes, 1)


def read_plane(plan, ref, c, k):
    rows = slice(c * plan.bx, (c + 1) * plan.bx)
    return jnp.concatenate([ref[i * plan.gy + k, rows] for i in range(plan.gx)], 0)


def write_plane(plan, ref, c, k, values):
    rows = slice(c * plan.bx, (c + 1) * plan.bx)
    for i in range(plan.gx):
        ref[i * plan.gy + k, rows] = values[i * plan.bx : (i + 1) * plan.bx]


def first_kernel(plan, held, field_ref, out_ref):
    planes = jnp.concatenate(
        [read_plane(plan, field_ref, c, k) for c in range(plan.cpd) for k in range(plan.gy)], 1
    )
    analyse_plane(plan, held, planes, plan.scale, out_ref)
    put_edges(plan, held, planes, out_ref, plan.mx)


def gelu_parts(z):
    factor = math.sqrt(2.0 / math.pi)
    tanh = jnp.tanh(factor * (z + 0.044715 * (z * z * z)))
    cdf = 0.5 * (1.0 + tanh)
    slope = cdf + 0.5 * z * (1.0 - tanh * tanh) * (factor * (1.0 + (3.0 * 0.044715) * (z * z)))
    return z * cdf, slope


def middle_kernel(plan, held, modes_ref, conv_ref, out_ref, z_ref, grads):
    lane = lax.broadcasted_iota(jnp.int32, (1, plan.gy * plan.lanes), 1)
    zero = jnp.logical_and(lane < plan.lanes, lax.rem(lane, plan.my) == 0)
    doubled = jnp.where(zero, 1.0, 2.0)
    syn = synthesise_plane(plan, held, modes_ref, doubled) * plan.scale
    for c in range(plan.cpd):
        for k in range(plan.gy):
            start = c * plan.ny + k * plan.by
            z = syn[:, start : start + plan.by] + read_plane(plan, conv_ref, c, k).astype(F32)
            z = z.astype(BF16)
            write_plane(plan, z_ref, c, k, z)
            slope = gelu_parts(z.astype(F32))[1]
            cot = read_plane(plan, conv_ref, plan.cpd + c, k).astype(F32)
            grads[:, start : start + plan.by] = (cot * slope).astype(BF16)
    planes = grads[...]
    analyse_plane(plan, held, planes, doubled * plan.scale, out_ref)
    put_edges(plan, held, planes, z_ref, plan.rows)


def last_kernel(plan, held, both_ref, out_ref):
    syn = synthesise_plane(plan, held, both_ref, None) * plan.scale
    syn = syn.astype(BF16)
    for c in range(plan.cpd):
        for k in range(plan.gy):
            start = c * plan.ny + k * plan.by
            write_plane(plan, out_ref, c, k, syn[:, start : start + plan.by])
    terms = both_ref[0, plan.mx :].astype(F32)
    for s in range(1, plan.devices):
        terms = terms + both_ref[s, plan.mx :].astype(F32)
    terms = terms.astype(BF16)
    for s in range(plan.devices):
        out_ref[s, plan.rows :] = terms


def gather_modes(plan, x_ref, flat, turned, j):
    s, half = plan.devices, plan.lanes // 2
    values = flat[pl.ds(j, s, stride=plan.mx), :]
    for c in range(plan.cpd):
        turned[j, pl.ds(c, s, stride=plan.cpd), :] = values[:, c * half : (c + 1) * half]


def spread(plan, x_ref, flat):
    flat[...] = x_ref[:, : plan.mx, :].astype(F32).reshape(plan.devices * plan.mx, plan.lanes)


def modes_to_rows(plan, x_ref, flat, turned, rows):
    spread(plan, x_ref, flat)
    for j in range(plan.mx):
        gather_modes(plan, x_ref, flat, turned, j)
        rows[j] = turned[j].T


def rows_to_modes(plan, values, turned, flat, j):
    s = plan.devices
    turned[j] = values.T
    parts = [turned[j, pl.ds(c, s, stride=plan.cpd), :] for c in range(plan.cpd)]
    flat[pl.ds(j, s, stride=plan.mx), :] = jnp.concatenate(parts, 1)


def group_mask(rows, groups, width):
    row = lax.broadcasted_iota(jnp.int32, (rows, groups * width), 0)
    lane = lax.broadcasted_iota(jnp.int32, (rows, groups * width), 1)
    return lax.rem(row, groups) == lax.div(lane, width)


def load_kernel(plan, *refs):
    count = len(refs) // 2
    copies = [pltpu.make_async_copy(refs[i], refs[count + i], refs[-1].at[i]) for i in range(count)]
    for copy in copies:
        copy.start()
    for copy in copies:
        copy.wait()


def each_mode_row(plan, product, r_ref, x_ref, y_ref, flat, turned, rows, held, sems):
    width = plan.channels
    copies = [
        pltpu.make_async_copy(
            r_ref.at[:, pl.ds(t * CHUNK, CHUNK)], held.at[:, pl.ds(t * CHUNK, CHUNK)], sems.at[t]
        )
        for t in range(plan.mx // CHUNK)
    ]
    for copy in copies:
        copy.start()
    modes_to_rows(plan, x_ref, flat, turned, rows)
    mask = group_mask(2 * GROUP, GROUP, width)
    for j in range(plan.mx):
        if j % CHUNK == 0:
            copies[j // CHUNK].wait()
        real_out, imag_out = [], []
        for g in range(plan.my // GROUP):
            start = g * GROUP
            real = rows[j, start : start + GROUP, :]
            imag = rows[j, plan.my + start : plan.my + start + GROUP, :]
            weights = [
                held[part, j, start : start + GROUP].reshape(GROUP * width, width)
                for part in range(2)
            ]
            real, imag = product(mask, real, imag, *weights)
            real_out.append(real)
            imag_out.append(imag)
        rows_to_modes(plan, jnp.concatenate(real_out + imag_out, 0), turned, flat, j)
    y_ref[...] = flat[...].reshape(plan.devices, plan.mx, plan.lanes).astype(BF16)


def mix_kernel(plan, held, *refs):
    def product(mask, real, imag, r_real, r_imag):
        first = jnp.concatenate([jnp.concatenate([real, imag], 0)] * GROUP, 1)
        second = jnp.concatenate([jnp.concatenate([-imag, real], 0)] * GROUP, 1)
        mixed = dot(jnp.where(mask, first, 0.0).astype(BF16), r_real)
        mixed = mixed + dot(jnp.where(mask, second, 0.0).astype(BF16), r_imag)
        return mixed[:GROUP], mixed[GROUP:]

    each_mode_row(plan, product, *refs)


def back_kernel(plan, held, *refs):
    width = plan.channels

    def product(mask, real, imag, r_real, r_imag):
        left = jnp.concatenate(
            [jnp.concatenate([real, imag], 1), jnp.concatenate([imag, -real], 1)], 0
        )
        weights = jnp.concatenate([r_real, r_imag], 1)
        mixed = jnp.where(mask, dot_nt(left.astype(BF16), weights), 0.0)
        total = mixed[:, : 2 * width]
        for i in range(1, GROUP // 2):
            total = total + mixed[:, 2 * i * width : 2 * (i + 1) * width]
        total = total[:, :width] + total[:, width:]
        return total[:GROUP], total[GROUP:]

    each_mode_row(plan, product, *refs)


def outer_kernel(
    plan, first_j, count, held, x_ref, g_ref, *refs
):
    out_ref, x_flat, g_flat, a_turned, g_turned, slots, sems = refs
    my, width = plan.my, plan.channels
    spread(plan, x_ref, x_flat)
    spread(plan, g_ref, g_flat)
    for j in range(first_j, first_j + count):
        gather_modes(plan, x_ref, x_flat, a_turned, j)
        gather_modes(plan, g_ref, g_flat, g_turned, j)
    lane = lax.rem(lax.broadcasted_iota(jnp.int32, (width, 2 * my), 1), my)
    copies = []
    for j in range(first_j, first_j + count):
        left = a_turned[j]
        g_rows = g_turned[j].T
        g_real, g_imag = g_rows[:my], g_rows[my:]
        right = jnp.concatenate(
            [jnp.concatenate([g_real, g_imag], 1), jnp.concatenate([g_imag, -g_real], 1)], 0
        ).astype(BF16)
        for g in range(my // GROUP):
            picked = jnp.concatenate(
                [jnp.where(lane == g * GROUP + l, left, 0.0) for l in range(GROUP)], 0
            ).astype(BF16)
            value = dot(picked, right).astype(BF16)
            for part in range(2):
                slots[part, j - first_j, g * GROUP : (g + 1) * GROUP] = value[
                    :, part * width : (part + 1) * width
                ].reshape(GROUP, width, width)
        if (j + 1) % CHUNK == 0:
            t = (j + 1 - first_j) // CHUNK - 1
            copies.append(
                pltpu.make_async_copy(
                    slots.at[:, pl.ds(t * CHUNK, CHUNK)],
                    out_ref.at[:, pl.ds(first_j + t * CHUNK, CHUNK)],
                    sems.at[t],
                )
            )
            copies[-1].start()
    for copy in copies:
        copy.wait()


def fill_taps(plan, block, edges, paired, taps):
    c, bx, by, s = plan.channels, plan.bx, plan.by, plan.devices

    def edge(first):
        for p in range(plan.cpd):
            paired[pl.ds(p, s, stride=plan.cpd), :] = edges[
                pl.ds(first + 2 * p, s, stride=EDGE), :
            ]
        return paired[...]

    top, bottom = edge(0), edge(1)
    left, right = edge(2 * plan.cpd), edge(2 * plan.cpd + 1)
    lane = lax.broadcasted_iota(jnp.int32, (c, by), 1)
    for x in range(bx + 2):
        if x == 0:
            row = top
        elif x == bx + 1:
            row = bottom
        else:
            row = block[pl.ds(x - 1, c, stride=bx), :]
        lanes = slice(x * by, (x + 1) * by)
        taps[:c, lanes] = jnp.where(
            lane == 0, left[:, x : x + 1], pltpu.roll(row, 1, 1)
        ).astype(BF16)
        taps[c : 2 * c, lanes] = row.astype(BF16)
        taps[2 * c :, lanes] = jnp.where(
            lane == by - 1, right[:, x : x + 1], pltpu.roll(row, by - 1, 1)
        ).astype(BF16)


def convolve(plan, weights, taps, out):
    bx, by = plan.bx, plan.by
    total = dot(weights[0], taps[:, : bx * by])
    for a in range(1, 3):
        total = total + dot(weights[a], taps[:, a * by : (a + bx) * by])
    for x in range(bx):
        out[pl.ds(x, plan.channels, stride=bx), :] = total[:, x * by : (x + 1) * by]


def conv_kernel(plan, held, both_ref, out_ref, block, edges, paired, taps):
    edges[...] = both_ref[:, plan.mx :, :].astype(F32).reshape(edges.shape)
    block[...] = held["field"][...].astype(F32).reshape(block.shape)
    fill_taps(plan, block, edges, paired, taps)
    kernel_ref = held["kernel"]
    weights = [jnp.concatenate([kernel_ref[a, b] for b in range(3)], 1) for a in range(3)]
    convolve(plan, weights, taps, block)
    out_ref[:, : plan.rows] = block[...].reshape(plan.devices, plan.rows, plan.by).astype(BF16)
    out_ref[:, plan.rows :] = held["cotangent"][...].reshape(plan.devices, plan.rows, plan.by)


def space_kernel(
    plan, held, z_ref, back_ref, layer_ref, grad_ref, both_ref, block, edges, paired, taps, flat
):
    c, bx, by, s = plan.channels, plan.bx, plan.by, plan.devices
    z = z_ref[:, : plan.rows, :].astype(F32).reshape(c, bx, by)
    activated, slope = gelu_parts(z)
    field = held["field"][...].astype(F32)
    layer_ref[...] = (field + activated).astype(BF16)
    block[...] = field.reshape(block.shape)
    for x in range(bx):
        flat[:, x * by : (x + 1) * by] = block[pl.ds(x, c, stride=bx), :].astype(BF16)
    cot_ref = held["cotangent"]
    grads = (cot_ref[...].astype(F32) * slope).astype(BF16).astype(F32)
    block[...] = grads.reshape(block.shape)
    edges[...] = z_ref[:, plan.rows :, :].astype(F32).reshape(edges.shape)
    fill_taps(plan, block, edges, paired, taps)
    kernel_ref = held["kernel"]
    weights = [
        jnp.concatenate(
            [kernel_ref[2 - a, 2 - b].astype(F32).T for b in range(3)], 1
        ).astype(BF16)
        for a in range(3)
    ]
    convolve(plan, weights, taps, block)
    grad_ref[...] = cot_ref[...].astype(F32) + block[...].reshape(c, bx, by)
    terms = jnp.concatenate(
        [dot_nt(taps[:, a * by : (a + bx) * by], flat[...]) for a in range(3)], 0
    )
    half = terms.shape[0] // 2
    terms = jnp.concatenate([terms[:half], terms[half:]], 1)
    edges[...] = jnp.zeros(edges.shape, F32)
    for t in range(half // s):
        edges[pl.ds(t, s, stride=EDGE), :] = terms[t * s : (t + 1) * s]
    both_ref[:, : plan.mx, :] = back_ref[...]
    both_ref[:, plan.mx :, :] = edges[...].reshape(s, EDGE, by).astype(BF16)


def end_kernel(plan, held, last_ref, grad_ref, out_ref, kernel_ref, edges):
    c, bx, by, s = plan.channels, plan.bx, plan.by, plan.devices
    edges[...] = last_ref[:, plan.rows :, :].astype(F32).reshape(edges.shape)
    count = 9 * c // (2 * s)
    for t in range(count):
        rows = edges[pl.ds(t, s, stride=EDGE), :]
        for h in range(2):
            start = (h * count + t) * s
            tap, first = start // c, start % c
            a, b = 2 - tap // 3, 2 - tap % 3
            kernel_ref[a, b, first : first + s, :] = rows[:, h * c : (h + 1) * c]
    syn = last_ref[:, : plan.rows, :].astype(F32).reshape(c, bx, by)
    out_ref[...] = (grad_ref[...] + syn).astype(BF16)


def fast_body(plan, field, spectral_weight, kernel_weight, cotangent):
    channels, bx, by, n, cpd = plan.channels, plan.bx, plan.by, plan.devices, plan.cpd
    anywhere = pl.BlockSpec(memory_space=pl.ANY)
    here = pl.BlockSpec(memory_space=pltpu.VMEM)

    def exchange(x):
        return lax.all_to_all(x, BOTH, 0, 0, tiled=True)

    def rows_of(count):
        return jax.ShapeDtypeStruct((n, count, by), BF16)

    def call(
        kernel, outs, *args, us=1.0, scratch=(), mib=56, raw=(), use=(), after=(), spec=None,
        alias=False,
    ):
        several = isinstance(outs, tuple)
        outs = outs if several else (outs,)
        steps = (len(raw), len(args), len(use), len(after))

        def run(*refs):
            groups = []
            for step in steps:
                groups.append(refs[:step])
                refs = refs[step:]
            kernel(plan, dict(zip(use, groups[2])), *groups[0], *groups[1], *refs)

        results = pl.pallas_call(
            run,
            out_shape=outs,
            in_specs=[anywhere] * len(raw)
            + [here] * (len(args) + len(use))
            + [anywhere] * len(after),
            out_specs=(spec or here,) * len(outs),
            scratch_shapes=scratch,
            input_output_aliases={sum(steps) - 1: 0} if alias else {},
            cost_estimate=pl.CostEstimate(
                flops=int(us * 1.0e9), bytes_accessed=1024, transcendentals=0
            ),
            compiler_params=pltpu.CompilerParams(vmem_limit_bytes=mib * 1024 * 1024),
        )(*raw, *args, *(held[name] for name in use), *after)
        return results if several else results[0]

    flat = pltpu.VMEM((n * plan.mx, plan.lanes), F32)
    turned = pltpu.VMEM((plan.mx, channels, 2 * plan.my), F32)
    rows = pltpu.VMEM((plan.mx, 2 * plan.my, channels), F32)
    block = pltpu.VMEM((channels * bx, by), F32)
    edges = pltpu.VMEM((n * EDGE, by), F32)
    paired = pltpu.VMEM((channels, by), F32)
    taps = pltpu.VMEM((3 * channels, (bx + 2) * by), BF16)
    field_flat = pltpu.VMEM((channels, bx * by), BF16)
    modes_scratch = [
        flat,
        turned,
        rows,
        pltpu.VMEM((2, plan.mx, plan.my, channels, channels), BF16),
        pltpu.SemaphoreType.DMA((plan.mx // CHUNK,)),
    ]
    edge_tables = ("pick_rows", "pick_cols", "window")

    field_c = exchange(field.reshape(n, plan.rows, by))
    sources = {name: jnp.asarray(t) for name, t in plan.named().items()}
    sources.update(field=field, cotangent=cotangent, kernel=kernel_weight)
    held = pl.pallas_call(
        partial(load_kernel, plan),
        out_shape=tuple(pltpu.VMEM(t.shape, t.dtype) for t in sources.values()),
        in_specs=[anywhere] * len(sources),
        out_specs=(here,) * len(sources),
        scratch_shapes=[pltpu.SemaphoreType.DMA((len(sources),))],
        cost_estimate=pl.CostEstimate(flops=2_500_000_000, bytes_accessed=1024, transcendentals=0),
        compiler_params=pltpu.CompilerParams(vmem_limit_bytes=60 * 1024 * 1024),
    )(*sources.values())
    held = dict(zip(sources, held))
    a_part = call(
        first_kernel,
        rows_of(plan.mx + EDGE),
        field_c,
        use=("col", "row") + edge_tables,
        mib=20,
    )
    a_both = exchange(a_part)
    conv = call(
        conv_kernel,
        rows_of(2 * plan.rows),
        a_both,
        use=("field", "cotangent", "kernel"),
        scratch=[block, edges, paired, taps],
        us=1.5,
        mib=20,
    )
    conv_c = exchange(conv)
    b_part = call(
        mix_kernel,
        rows_of(plan.mx),
        a_both,
        raw=(spectral_weight,),
        scratch=modes_scratch,
        us=6.5,
        after=(conv,),
    )
    b_part, conv_c = lax.optimization_barrier((b_part, conv_c))
    b_modes = exchange(b_part)
    g_part, z_part = call(
        middle_kernel,
        (rows_of(plan.mx), rows_of(plan.rows + EDGE)),
        b_modes,
        conv_c,
        use=("row_s", "col", "row") + edge_tables,
        mib=20,
        scratch=[pltpu.VMEM((plan.nx, cpd * plan.ny), BF16)],
        us=2.6,
    )
    g_modes = exchange(g_part)
    z_both = exchange(z_part)
    back_part = call(
        back_kernel,
        rows_of(plan.mx),
        g_modes,
        raw=(spectral_weight,),
        scratch=modes_scratch,
        us=6.5,
        after=(z_part,),
    )
    layer_out, grad_sum, back_terms = call(
        space_kernel,
        (
            jax.ShapeDtypeStruct(field.shape, BF16),
            jax.ShapeDtypeStruct(field.shape, F32),
            rows_of(plan.mx + EDGE),
        ),
        z_both,
        back_part,
        use=("field", "cotangent", "kernel"),
        mib=20,
        scratch=[block, edges, paired, taps, field_flat],
        us=3.8,
    )
    back_both = exchange(back_terms)

    def outer_part(first_j, count, after, alias):
        return call(
            lambda plan, *refs: outer_kernel(plan, first_j, count, *refs),
            jax.ShapeDtypeStruct(spectral_weight.shape, BF16),
            a_both,
            g_modes,
            scratch=[
                flat,
                flat,
                turned,
                turned,
                pltpu.VMEM((2, count, plan.my, channels, channels), BF16),
                pltpu.SemaphoreType.DMA((count // CHUNK,)),
            ],
            spec=anywhere,
            us=6.4,
            after=after,
            alias=alias,
        )

    half = plan.mx // 2
    spectral_half = outer_part(0, half, (back_terms,), False)
    last_part = call(
        last_kernel,
        rows_of(plan.rows + EDGE),
        back_both,
        use=("row_s", "col"),
        us=1.3,
        mib=44,
        after=(spectral_half,),
    )
    last_both = exchange(last_part)
    spectral_grad = outer_part(half, half, (last_part, spectral_half), True)
    field_grad, kernel_grad = call(
        end_kernel,
        (
            jax.ShapeDtypeStruct(field.shape, BF16),
            jax.ShapeDtypeStruct((3, 3, channels, channels), F32),
        ),
        last_both,
        grad_sum,
        scratch=[edges],
        mib=20,
    )
    return (layer_out, field_grad, spectral_grad, kernel_grad)


def body(field, spectral_weight, kernel_weight, cotangent):
    plan = Plan(*field.shape, lax.axis_size("gx"), lax.axis_size("gy"))
    if plan.fits:
        return fast_body(plan, field, spectral_weight, kernel_weight, cotangent)
    return general_body(field, spectral_weight, kernel_weight, cotangent)


def solution(mesh):
    in_specs = (P(None, "gx", "gy"), P(None, "gx", "gy", None, None), P(), P(None, "gx", "gy"))
    out_specs = (P(None, "gx", "gy"), P(None, "gx", "gy"), P(None, "gx", "gy", None, None), P())
    return jax.shard_map(body, mesh=mesh, in_specs=in_specs, out_specs=out_specs, check_vma=False)
```

```python
from functools import partial
import math

import jax
import jax.numpy as jnp
import ml_dtypes
import numpy as np
from jax import lax
from jax.experimental import pallas as pl
from jax.experimental.pallas import tpu as pltpu
from jax.sharding import PartitionSpec as P

KX = 128
KY = 128


def extended(array, sides, width):
    for axis, dim in sides:
        count, length = (lax.axis_size(axis), array.shape[dim])
        up = [(i, (i + 1) % count) for i in range(count)]
        down = [(j, i) for i, j in up]
        last = lax.slice_in_dim(array, length - width, length, axis=dim)
        initial = lax.slice_in_dim(array, 0, width, axis=dim)
        before = lax.ppermute(last, axis, up)
        after = lax.ppermute(initial, axis, down)
        array = jnp.concatenate([before, array, after], axis=dim)
    return array


def phases(waves, points, length):
    wrapped = jnp.mod(waves[:, None] * points[None, :], length).astype(jnp.float32)
    return wrapped * (2.0 * math.pi / length)


def widen(field):
    return extended(field, (("gx", 1), ("gy", 2)), 1)


def general_body(field, spectral_weight, kernel_weight, cotangent):
    highest = lax.Precision.HIGHEST
    channels, block_rows, block_cols = field.shape
    rows_total = block_rows * lax.axis_size("gx")
    cols_total = block_cols * lax.axis_size("gy")
    scale = 1.0 / math.sqrt(rows_total * cols_total)
    row_coord = lax.axis_index("gx") * block_rows + jnp.arange(block_rows, dtype=jnp.int32)
    col_coord = lax.axis_index("gy") * block_cols + jnp.arange(block_cols, dtype=jnp.int32)
    modes_x = KX // lax.axis_size("gx")
    modes_y = KY // lax.axis_size("gy")

    def analyse(source):
        waves = jnp.arange(lax.axis_size("gy") * modes_y, dtype=jnp.int32)
        angles = phases(waves, col_coord, cols_total)
        table = jnp.concatenate([jnp.cos(angles), -jnp.sin(angles)], 0).astype(jnp.bfloat16)
        product = jnp.dot(
            source.reshape(channels * block_rows, block_cols),
            table.T,
            preferred_element_type=jnp.float32,
        )
        product = product.reshape(channels, block_rows, 2, lax.axis_size("gy") * modes_y).transpose(
            3, 1, 2, 0
        )
        col_modes = lax.psum_scatter(
            product.reshape(lax.axis_size("gy") * modes_y, block_rows, 2 * channels),
            "gy",
            scatter_dimension=0,
            tiled=True,
        )
        split_modes = col_modes.reshape(modes_y, block_rows, 2, channels)
        real_in = split_modes[:, :, 0]
        imag_in = split_modes[:, :, 1]
        waves = jnp.arange(lax.axis_size("gx") * modes_x, dtype=jnp.int32) - KX // 2
        angles = phases(waves, row_coord, rows_total)
        cosines = jnp.cos(angles)
        sines = jnp.sin(angles)
        contract = partial(jnp.einsum, "jx,lxc->jlc", precision=highest)
        real_out = contract(cosines, real_in) + contract(sines, imag_in)
        imag_out = contract(cosines, imag_in) - contract(sines, real_in)
        return lax.psum_scatter(
            jnp.stack([real_out, imag_out], 2).reshape(
                lax.axis_size("gx") * modes_x, modes_y, 2 * channels
            )
            * scale,
            "gx",
            scatter_dimension=0,
            tiled=True,
        ).reshape(modes_x, modes_y, 2, channels)

    def synthesise(modes):
        start_rows = jnp.zeros((modes_y, block_rows, 2 * channels), jnp.float32)
        shard_rows = lax.all_gather(
            modes.reshape(modes_x, modes_y, 2 * channels), "gx", axis=0, tiled=True
        )
        amount = shard_rows.shape[0]
        waves = jnp.arange(amount, dtype=jnp.int32) - KX // 2
        angles = phases(waves, row_coord, rows_total)
        cosines = jnp.cos(angles).astype(jnp.bfloat16)
        sines = jnp.sin(angles).astype(jnp.bfloat16)
        split_rows = shard_rows.reshape(amount, modes_y, 2, channels)
        real_in = split_rows[:, :, 0]
        imag_in = split_rows[:, :, 1]
        contract = partial(jnp.einsum, "jx,jlc->lxc", preferred_element_type=jnp.float32)
        real_out = contract(cosines, real_in) - contract(sines, imag_in)
        imag_out = contract(sines, real_in) + contract(cosines, imag_in)
        row_sum = start_rows + jnp.stack([real_out, imag_out], 2).reshape(
            modes_y, block_rows, 2 * channels
        )
        row_sum = row_sum.astype(jnp.bfloat16)
        shard_rows = lax.all_gather(row_sum, "gy", axis=0, tiled=True)
        amount = shard_rows.shape[0]
        waves = jnp.arange(amount, dtype=jnp.int32)
        angles = phases(waves, col_coord, cols_total)
        table = jnp.stack([jnp.cos(angles), -jnp.sin(angles)], 1).astype(jnp.bfloat16)
        split_rows = shard_rows.reshape(amount, block_rows, 2, channels)
        return (
            jnp.einsum("lxpc,lpy->cxy", split_rows, table, preferred_element_type=jnp.float32)
            * scale
        )

    padded_field = widen(field)
    hidden = jnp.zeros((channels, block_rows, block_cols), jnp.float32)
    for row_tap in range(3):
        for col_tap in range(3):
            window = padded_field[:, row_tap : row_tap + block_rows, col_tap : col_tap + block_cols]
            hidden = hidden + jnp.einsum(
                "oi,ixy->oxy",
                kernel_weight[row_tap, col_tap],
                window,
                preferred_element_type=jnp.float32,
            )
    amodes = analyse(field)
    areal = amodes[:, :, 0]
    aimag = amodes[:, :, 1]
    wreal = spectral_weight[0].astype(jnp.float32)
    wimag = spectral_weight[1].astype(jnp.float32)
    mixing = partial(jnp.einsum, "jli,jlio->jlo", precision=highest)
    breal = mixing(areal, wreal) - mixing(aimag, wimag)
    bimag = mixing(areal, wimag) + mixing(aimag, wreal)
    wave_index = lax.axis_index("gy") * modes_y + jnp.arange(modes_y, dtype=jnp.int32)
    weights = jnp.where(wave_index == 0, 1.0, 2.0).astype(jnp.float32)[None, :, None, None]
    bmodes = (jnp.stack([breal, bimag], 2) * weights).astype(jnp.bfloat16)
    hidden = hidden + synthesise(bmodes)
    activated, pullback = jax.vjp(jax.nn.gelu, hidden)
    layer_out = (field.astype(jnp.float32) + activated).astype(jnp.bfloat16)
    grads = pullback(cotangent.astype(jnp.float32))[0].astype(jnp.bfloat16)
    gmodes = analyse(grads) * weights
    greal = gmodes[:, :, 0]
    gimag = gmodes[:, :, 1]
    outer = partial(jnp.einsum, "jli,jlo->jlio", precision=highest)
    spectral_grad = jnp.stack(
        [outer(areal, greal) + outer(aimag, gimag), outer(areal, gimag) - outer(aimag, greal)], 0
    ).astype(jnp.bfloat16)
    back = partial(jnp.einsum, "jlio,jlo->jli", precision=highest)
    back_real = back(wreal, greal) + back(wimag, gimag)
    back_imag = back(wreal, gimag) - back(wimag, greal)
    back_modes = jnp.stack([back_real, back_imag], 2).astype(jnp.bfloat16)
    padded_grads = widen(grads)
    adjoint = jnp.zeros((channels, block_rows, block_cols), jnp.float32)
    tap_rows = []
    for row_tap in range(3):
        tap_cols = []
        for col_tap in range(3):
            window = padded_grads[
                :, 2 - row_tap : 2 - row_tap + block_rows, 2 - col_tap : 2 - col_tap + block_cols
            ]
            adjoint = adjoint + jnp.einsum(
                "oi,oxy->ixy",
                kernel_weight[row_tap, col_tap],
                window,
                preferred_element_type=jnp.float32,
            )
            source_window = padded_field[
                :, row_tap : row_tap + block_rows, col_tap : col_tap + block_cols
            ]
            tap_cols.append(
                jnp.einsum("oxy,ixy->oi", grads, source_window, preferred_element_type=jnp.float32)
            )
        tap_rows.append(jnp.stack(tap_cols, 0))
    kernel_grad = lax.psum(jnp.stack(tap_rows, 0), ("gx", "gy"))
    field_grad = (cotangent.astype(jnp.float32) + adjoint + synthesise(back_modes)).astype(
        jnp.bfloat16
    )
    return (layer_out, field_grad, spectral_grad, kernel_grad)


BF16 = jnp.bfloat16
F32 = jnp.float32
BOTH = ("gx", "gy")
EDGE = 16
GROUP = 8
CHUNK = 2
MIXED = 8


class Plan:
    def __init__(self, channels, block_rows, block_cols, gx, gy):
        self.gx, self.gy, self.devices = gx, gy, gx * gy
        self.channels, self.bx, self.by = channels, block_rows, block_cols
        self.nx, self.ny = block_rows * gx, block_cols * gy
        self.mx, self.my = KX // gx, KY // gy
        self.cpd = channels // self.devices if channels % self.devices == 0 else 0
        self.lanes = self.cpd * 2 * self.my
        self.rows = self.cpd * self.bx
        self.fits = (
            self.cpd == 2
            and channels == 64
            and self.lanes == 128
            and self.by == 128
            and self.bx == 16
            and KX % gx == 0
            and KY % gy == 0
            and self.mx == 16
            and self.my % GROUP == 0
            and gy % 2 == 0
            and KX == 128
            and self.nx == 128
        )
        self.scale = 1.0 / math.sqrt(self.nx * self.ny)

    def tables(self):
        two_pi = np.float32(2.0 * math.pi)
        waves, points = np.arange(KY), np.arange(self.ny)
        angles = np.float32((waves[:, None] * points[None, :]) % self.ny) * (two_pi / self.ny)
        cos, sin = np.cos(angles).T, np.sin(angles).T
        split = (self.ny, self.gy, self.my)
        cos, sin = cos.reshape(split), sin.reshape(split)
        top, bottom = np.stack([cos, -sin], 2), np.stack([-sin, -cos], 2)
        col = np.stack([top, bottom], 1).reshape(self.ny, -1).astype(ml_dtypes.bfloat16)
        rows = np.arange(KX) - KX // 2
        points = np.arange(self.nx)
        angles = np.float32((rows[:, None] * points[None, :]) % self.nx) * (two_pi / self.nx)
        row = np.concatenate([np.cos(angles), np.sin(angles)], 1).astype(np.float32)
        high = row.astype(ml_dtypes.bfloat16)
        low = (row - high.astype(np.float32)).astype(ml_dtypes.bfloat16)
        row_analysis = np.concatenate([high, low], 1)
        row_synthesis = np.concatenate([np.cos(angles).T, np.sin(angles).T], 0)
        row_synthesis = row_synthesis.astype(ml_dtypes.bfloat16)
        return col, row_analysis, row_synthesis

    def named(self):
        names = ("col", "row", "row_s", "pick_rows", "pick_cols", "window")
        return dict(zip(names, self.tables() + self.pickers()))

    def pickers(self):
        pick_rows = np.zeros((self.gx, EDGE, self.cpd, self.nx), np.float32)
        pick_cols = np.zeros((self.gy, EDGE, self.cpd, self.ny), np.float32)
        window = np.zeros((self.nx, self.gx, self.by), np.float32)
        for c in range(self.cpd):
            for g in range(self.gx):
                pick_rows[g, 2 * c, c, (g * self.bx - 1) % self.nx] = 1
                pick_rows[g, 2 * c + 1, c, ((g + 1) * self.bx) % self.nx] = 1
            for g in range(self.gy):
                pick_cols[g, 2 * self.cpd + 2 * c, c, (g * self.by - 1) % self.ny] = 1
                pick_cols[g, 2 * self.cpd + 2 * c + 1, c, ((g + 1) * self.by) % self.ny] = 1
        for g in range(self.gx):
            for t in range(self.bx + 2):
                window[(g * self.bx - 1 + t) % self.nx, g, t] = 1
        kind = ml_dtypes.bfloat16
        return (
            pick_rows.reshape(self.gx * EDGE, -1).astype(kind),
            pick_cols.reshape(self.gy * EDGE, -1).astype(kind),
            window.reshape(self.nx, -1).astype(kind),
        )


def dot(a, b):
    return jnp.dot(a, b, preferred_element_type=F32)


def dot_nt(a, b):
    return lax.dot_general(a, b, (((1,), (1,)), ((), ())), preferred_element_type=F32)


def interleave(plan, parts):
    half = plan.lanes // 2
    lane = lax.broadcasted_iota(jnp.int32, (1, plan.lanes), 1)
    tiles = []
    for k in range(plan.gy // 2):
        first, second = (p[:, k * plan.lanes : (k + 1) * plan.lanes] for p in parts)
        tiles.append(jnp.where(lane < half, first, pltpu.roll(second, half, 1)))
        tiles.append(jnp.where(lane < half, pltpu.roll(first, half, 1), second))
    return jnp.concatenate(tiles, 1)


def separate(plan, values):
    half = plan.lanes // 2
    lane = lax.broadcasted_iota(jnp.int32, (1, plan.lanes), 1)
    parts = ([], [])
    for k in range(plan.gy // 2):
        even = values[:, 2 * k * plan.lanes : (2 * k + 1) * plan.lanes]
        odd = values[:, (2 * k + 1) * plan.lanes : (2 * k + 2) * plan.lanes]
        parts[0].append(jnp.where(lane < half, even, pltpu.roll(odd, half, 1)))
        parts[1].append(jnp.where(lane < half, pltpu.roll(even, half, 1), odd))
    return [jnp.concatenate(p, 1) for p in parts]


def analyse_plane(plan, held, planes, weight, out_ref):
    col = held["col"]
    half = col.shape[1] // 2
    along_y = [
        dot(planes[:, c * plan.ny : (c + 1) * plan.ny], col[...]) for c in range(plan.cpd)
    ]
    stacked = jnp.concatenate(
        [
            interleave(plan, [p[:, :half] for p in along_y]),
            interleave(plan, [p[:, half:] for p in along_y]),
        ],
        0,
    ).astype(BF16)
    modes = dot(held["row"][...], jnp.concatenate([stacked, stacked], 0)) * weight
    modes = modes.astype(BF16)
    for i in range(plan.gx):
        for k in range(plan.gy):
            out_ref[i * plan.gy + k, : plan.mx] = modes[
                i * plan.mx : (i + 1) * plan.mx, k * plan.lanes : (k + 1) * plan.lanes
            ]


def put_edges(plan, held, planes, out_ref, start):
    stacked = jnp.concatenate(
        [planes[:, c * plan.ny : (c + 1) * plan.ny] for c in range(plan.cpd)], 0
    )
    edge_rows = dot(held["pick_rows"][...], stacked)
    picked = dot_nt(held["pick_cols"][...], planes).astype(BF16)
    edge_cols = dot(picked, held["window"][...])
    for i in range(plan.gx):
        for k in range(plan.gy):
            tile = (
                edge_rows[i * EDGE : (i + 1) * EDGE, k * plan.by : (k + 1) * plan.by]
                + edge_cols[k * EDGE : (k + 1) * EDGE, i * plan.by : (i + 1) * plan.by]
            )
            out_ref[i * plan.gy + k, start : start + EDGE] = tile.astype(BF16)


def synthesise_plane(plan, held, modes_ref, weight):
    columns = []
    for k in range(plan.gy):
        columns.append(
            jnp.concatenate([modes_ref[i * plan.gy + k, : plan.mx] for i in range(plan.gx)], 0)
        )
    sums = dot(held["row_s"][...], jnp.concatenate(columns, 1))
    if weight is not None:
        sums = sums * weight
    top, bottom = separate(plan, sums[: plan.nx]), separate(plan, sums[plan.nx :])
    planes = []
    for c in range(plan.cpd):
        left = jnp.concatenate([top[c], bottom[c]], 1).astype(BF16)
        planes.append(dot_nt(left, held["col"][...]))
    return jnp.concatenate(planes, 1)


def read_plane(plan, ref, c, k, first=0):
    rows = slice(first + c * plan.bx, first + (c + 1) * plan.bx)
    return jnp.concatenate([ref[i * plan.gy + k, rows] for i in range(plan.gx)], 0)


def write_plane(plan, ref, c, k, values, first=0):
    rows = slice(first + c * plan.bx, first + (c + 1) * plan.bx)
    for i in range(plan.gx):
        ref[i * plan.gy + k, rows] = values[i * plan.bx : (i + 1) * plan.bx]


def first_kernel(plan, held, field_ref, out_ref):
    planes = jnp.concatenate(
        [read_plane(plan, field_ref, c, k) for c in range(plan.cpd) for k in range(plan.gy)], 1
    )
    analyse_plane(plan, held, planes, plan.scale, out_ref)
    put_edges(plan, held, planes, out_ref, plan.mx)


def gelu_parts(z):
    factor = math.sqrt(2.0 / math.pi)
    tanh = jnp.tanh(factor * (z + 0.044715 * (z * z * z)))
    cdf = 0.5 * (1.0 + tanh)
    slope = cdf + 0.5 * z * (1.0 - tanh * tanh) * (factor * (1.0 + (3.0 * 0.044715) * (z * z)))
    return z * cdf, slope


def middle_kernel(plan, held, modes_ref, out_ref, grads):
    lane = lax.broadcasted_iota(jnp.int32, (1, plan.gy * plan.lanes), 1)
    zero = jnp.logical_and(lane < plan.lanes, lax.rem(lane, plan.my) == 0)
    doubled = jnp.where(zero, 1.0, 2.0)
    syn = synthesise_plane(plan, held, modes_ref, doubled) * plan.scale
    for c in range(plan.cpd):
        for k in range(plan.gy):
            start = c * plan.ny + k * plan.by
            z = syn[:, start : start + plan.by] + read_plane(plan, modes_ref, c, k, plan.mx).astype(F32)
            z = z.astype(BF16)
            write_plane(plan, out_ref, c, k, z, plan.mx)
            slope = gelu_parts(z.astype(F32))[1]
            cot = read_plane(plan, modes_ref, plan.cpd + c, k, plan.mx).astype(F32)
            grads[:, start : start + plan.by] = (cot * slope).astype(BF16)
    planes = grads[...]
    analyse_plane(plan, held, planes, doubled * plan.scale, out_ref)
    put_edges(plan, held, planes, out_ref, plan.mx + plan.rows)


def last_kernel(plan, held, both_ref, out_ref):
    syn = synthesise_plane(plan, held, both_ref, None) * plan.scale
    syn = syn.astype(BF16)
    for c in range(plan.cpd):
        for k in range(plan.gy):
            start = c * plan.ny + k * plan.by
            write_plane(plan, out_ref, c, k, syn[:, start : start + plan.by])
    terms = both_ref[0, plan.mx :].astype(F32)
    for s in range(1, plan.devices):
        terms = terms + both_ref[s, plan.mx :].astype(F32)
    terms = terms.astype(BF16)
    for s in range(plan.devices):
        out_ref[s, plan.rows :] = terms


def gather_modes(plan, x_ref, flat, turned, j):
    s, half = plan.devices, plan.lanes // 2
    values = flat[pl.ds(j, s, stride=plan.mx), :]
    for c in range(plan.cpd):
        turned[j, pl.ds(c, s, stride=plan.cpd), :] = values[:, c * half : (c + 1) * half]


def spread(plan, x_ref, flat):
    flat[...] = x_ref[:, : plan.mx, :].astype(F32).reshape(plan.devices * plan.mx, plan.lanes)


def modes_to_rows(plan, x_ref, flat, turned, rows):
    spread(plan, x_ref, flat)
    for j in range(plan.mx):
        gather_modes(plan, x_ref, flat, turned, j)
        rows[j] = turned[j].T


def rows_to_modes(plan, values, turned, flat, j):
    s = plan.devices
    turned[j] = values.T
    parts = [turned[j, pl.ds(c, s, stride=plan.cpd), :] for c in range(plan.cpd)]
    flat[pl.ds(j, s, stride=plan.mx), :] = jnp.concatenate(parts, 1)


def group_mask(rows, groups, width):
    row = lax.broadcasted_iota(jnp.int32, (rows, groups * width), 0)
    lane = lax.broadcasted_iota(jnp.int32, (rows, groups * width), 1)
    return lax.rem(row, groups) == lax.div(lane, width)


def pack_rows(plan, first_j, count, r_ref, packed_ref, arrived, packed, in_sems, out_sems, others=()):
    chunks = count // CHUNK

    def part(t, start=0):
        return pl.ds(start + t * CHUNK, CHUNK)

    loads = [
        pltpu.make_async_copy(r_ref.at[:, part(t, first_j)], arrived.at[:, part(t)], in_sems.at[t])
        for t in range(chunks)
    ]
    stores = [
        pltpu.make_async_copy(packed.at[part(t)], packed_ref.at[part(t, first_j)], out_sems.at[t])
        for t in range(chunks)
    ]
    for copy in loads + list(others):
        copy.start()
    for t in range(chunks):
        loads[t].wait()
        for j in range(t * CHUNK, (t + 1) * CHUNK):
            packed[j] = jnp.concatenate([arrived[0, j], arrived[1, j]], -1)
        stores[t].start()
    for copy in list(others) + stores:
        copy.wait()


def load_kernel(plan, half, *refs):
    count = (len(refs) - 7) // 2
    r_ref, sources = refs[0], refs[1 : 1 + count]
    packed_ref, places = refs[1 + count], refs[2 + count : 2 + 2 * count]
    arrived, packed, sems, in_sems, out_sems = refs[2 + 2 * count :]
    copies = [
        pltpu.make_async_copy(source, place, sems.at[i])
        for i, (source, place) in enumerate(zip(sources, places))
    ]
    pack_rows(plan, 0, half, r_ref, packed_ref, arrived, packed, in_sems, out_sems, copies)


def each_mode_row(plan, product, first, r_ref, x_ref, y_ref, flat, turned, rows, held, sems):
    width = plan.channels
    copies = [
        pltpu.make_async_copy(
            r_ref.at[pl.ds(t * MIXED, MIXED)], held.at[pl.ds(t * MIXED, MIXED)], sems.at[t]
        )
        for t in range(plan.mx // MIXED)
    ]
    for copy in copies:
        copy.start()
    modes_to_rows(plan, x_ref, flat, turned, rows)
    first()
    mask = group_mask(2 * GROUP, GROUP, width)

    def step(j, carry):
        real_out, imag_out = [], []
        for g in range(plan.my // GROUP):
            start = g * GROUP
            real = rows[j, start : start + GROUP, :]
            imag = rows[j, plan.my + start : plan.my + start + GROUP, :]
            weights = held[j, start : start + GROUP].reshape(GROUP * width, 2 * width)
            real, imag = product(mask, real, imag, weights)
            real_out.append(real)
            imag_out.append(imag)
        rows_to_modes(plan, jnp.concatenate(real_out + imag_out, 0), turned, flat, j)
        return carry

    for t, copy in enumerate(copies):
        copy.wait()
        lax.fori_loop(t * MIXED, (t + 1) * MIXED, step, 0, unroll=8)
    values = flat[...].reshape(plan.devices, plan.mx, plan.lanes)
    y_ref[:, : plan.mx] = values.astype(BF16)


class Arrival:
    def __init__(self, source, place, sem):
        self.copy, self.place, self.there = pltpu.make_async_copy(source, place, sem), place, False
        self.copy.start()

    def __getitem__(self, index):
        if not self.there:
            self.copy.wait()
            self.there = True
        return self.place[index]


def bring(sources, refs):
    count = len(sources)
    arrivals = {
        name: Arrival(source, refs[i], refs[count].at[i])
        for i, (name, source) in enumerate(sources)
    }
    return arrivals, refs[count + 1 :]


def mix_kernel(plan, held, r_ref, field_ref, cot_ref, kernel_ref, x_ref, y_ref, *refs):
    width = plan.channels
    held, refs = bring((("field", field_ref), ("kernel", kernel_ref)), refs)
    cot = pltpu.make_async_copy(cot_ref, y_ref.at[:, pl.ds(plan.mx + plan.rows, plan.rows)], refs[-1])
    cot.start()
    refs = refs[:-1]

    def product(mask, real, imag, weights):
        left = jnp.concatenate([jnp.concatenate([real, imag], 0)] * GROUP, 1)
        mixed = dot(jnp.where(mask, left, 0.0).astype(BF16), weights)
        return (
            mixed[:GROUP, :width] - mixed[GROUP:, width:],
            mixed[:GROUP, width:] + mixed[GROUP:, :width],
        )

    conv = partial(conv_part, plan, held, x_ref, y_ref, *refs[:4])
    each_mode_row(plan, product, conv, r_ref, x_ref, y_ref, *refs[4:])
    cot.wait()


def back_kernel(
    plan, held, r_ref, field_ref, cot_ref, kernel_ref, g_ref, layer_ref, grad_ref, both_ref, *refs
):
    width = plan.channels
    sources = (("field", field_ref), ("cotangent", cot_ref), ("kernel", kernel_ref))
    held, refs = bring(sources, refs)

    def product(mask, real, imag, weights):
        left = jnp.concatenate(
            [jnp.concatenate([real, imag], 1), jnp.concatenate([imag, -real], 1)], 0
        )
        mixed = jnp.where(mask, dot_nt(left.astype(BF16), weights), 0.0)
        total = mixed[:, : 2 * width]
        for i in range(1, GROUP // 2):
            total = total + mixed[:, 2 * i * width : 2 * (i + 1) * width]
        total = total[:, :width] + total[:, width:]
        return total[:GROUP], total[GROUP:]

    space = partial(space_part, plan, held, g_ref, layer_ref, grad_ref, both_ref, *refs[:5])
    each_mode_row(plan, product, space, r_ref, g_ref, both_ref, *refs[5:])


def outer_kernel(
    plan, first_j, count, held, x_ref, g_ref, *refs
):
    out_ref, x_flat, g_flat, a_turned, g_turned, slots, sems = refs
    my, width = plan.my, plan.channels
    spread(plan, x_ref, x_flat)
    spread(plan, g_ref, g_flat)
    for j in range(first_j, first_j + count):
        gather_modes(plan, x_ref, x_flat, a_turned, j)
        gather_modes(plan, g_ref, g_flat, g_turned, j)
    lane = lax.rem(lax.broadcasted_iota(jnp.int32, (width, 2 * my), 1), my)
    copies = []
    for j in range(first_j, first_j + count):
        left = a_turned[j]
        g_rows = g_turned[j].T
        g_real, g_imag = g_rows[:my], g_rows[my:]
        right = jnp.concatenate(
            [jnp.concatenate([g_real, g_imag], 1), jnp.concatenate([g_imag, -g_real], 1)], 0
        ).astype(BF16)
        for g in range(my // GROUP):
            picked = jnp.concatenate(
                [jnp.where(lane == g * GROUP + l, left, 0.0) for l in range(GROUP)], 0
            ).astype(BF16)
            value = dot(picked, right).astype(BF16)
            for part in range(2):
                slots[part, j - first_j, g * GROUP : (g + 1) * GROUP] = value[
                    :, part * width : (part + 1) * width
                ].reshape(GROUP, width, width)
        if (j + 1) % CHUNK == 0:
            t = (j + 1 - first_j) // CHUNK - 1
            copies.append(
                pltpu.make_async_copy(
                    slots.at[:, pl.ds(t * CHUNK, CHUNK)],
                    out_ref.at[:, pl.ds(first_j + t * CHUNK, CHUNK)],
                    sems.at[t],
                )
            )
            copies[-1].start()
    for copy in copies:
        copy.wait()


def fill_taps(plan, block, edges, paired, taps):
    c, bx, by, s = plan.channels, plan.bx, plan.by, plan.devices

    def edge(first):
        for p in range(plan.cpd):
            paired[pl.ds(p, s, stride=plan.cpd), :] = edges[
                pl.ds(first + 2 * p, s, stride=EDGE), :
            ]
        return paired[...]

    top, bottom = edge(0), edge(1)
    left, right = edge(2 * plan.cpd), edge(2 * plan.cpd + 1)
    lane = lax.broadcasted_iota(jnp.int32, (c, by), 1)
    for x in range(bx + 2):
        if x == 0:
            row = top
        elif x == bx + 1:
            row = bottom
        else:
            row = block[pl.ds(x - 1, c, stride=bx), :]
        lanes = slice(x * by, (x + 1) * by)
        taps[:c, lanes] = jnp.where(
            lane == 0, left[:, x : x + 1], pltpu.roll(row, 1, 1)
        ).astype(BF16)
        taps[c : 2 * c, lanes] = row.astype(BF16)
        taps[2 * c :, lanes] = jnp.where(
            lane == by - 1, right[:, x : x + 1], pltpu.roll(row, by - 1, 1)
        ).astype(BF16)


def convolve(plan, weights, taps, out):
    bx, by = plan.bx, plan.by
    total = dot(weights[0], taps[:, : bx * by])
    for a in range(1, 3):
        total = total + dot(weights[a], taps[:, a * by : (a + bx) * by])
    for x in range(bx):
        out[pl.ds(x, plan.channels, stride=bx), :] = total[:, x * by : (x + 1) * by]


def conv_part(plan, held, both_ref, out_ref, block, edges, paired, taps):
    edges[...] = both_ref[:, plan.mx :, :].astype(F32).reshape(edges.shape)
    block[...] = held["field"][...].astype(F32).reshape(block.shape)
    fill_taps(plan, block, edges, paired, taps)
    kernel_ref = held["kernel"]
    weights = [jnp.concatenate([kernel_ref[a, b] for b in range(3)], 1) for a in range(3)]
    convolve(plan, weights, taps, block)
    shape = (plan.devices, plan.rows, plan.by)
    out_ref[:, plan.mx : plan.mx + plan.rows] = block[...].reshape(shape).astype(BF16)


def space_part(
    plan, held, z_ref, layer_ref, grad_ref, both_ref, block, edges, paired, taps, flat
):
    c, bx, by, s = plan.channels, plan.bx, plan.by, plan.devices
    z = z_ref[:, plan.mx : plan.mx + plan.rows, :].astype(F32).reshape(c, bx, by)
    activated, slope = gelu_parts(z)
    field = held["field"][...].astype(F32)
    layer_ref[...] = (field + activated).astype(BF16)
    block[...] = field.reshape(block.shape)
    for x in range(bx):
        flat[:, x * by : (x + 1) * by] = block[pl.ds(x, c, stride=bx), :].astype(BF16)
    cot_ref = held["cotangent"]
    grads = (cot_ref[...].astype(F32) * slope).astype(BF16).astype(F32)
    block[...] = grads.reshape(block.shape)
    edges[...] = z_ref[:, plan.mx + plan.rows :, :].astype(F32).reshape(edges.shape)
    fill_taps(plan, block, edges, paired, taps)
    kernel_ref = held["kernel"]
    weights = [
        jnp.concatenate(
            [kernel_ref[2 - a, 2 - b].astype(F32).T for b in range(3)], 1
        ).astype(BF16)
        for a in range(3)
    ]
    convolve(plan, weights, taps, block)
    grad_ref[...] = cot_ref[...].astype(F32) + block[...].reshape(c, bx, by)
    terms = jnp.concatenate(
        [dot_nt(taps[:, a * by : (a + bx) * by], flat[...]) for a in range(3)], 0
    )
    half = terms.shape[0] // 2
    terms = jnp.concatenate([terms[:half], terms[half:]], 1)
    edges[...] = jnp.zeros(edges.shape, F32)
    for t in range(half // s):
        edges[pl.ds(t, s, stride=EDGE), :] = terms[t * s : (t + 1) * s]
    both_ref[:, plan.mx :, :] = edges[...].reshape(s, EDGE, by).astype(BF16)


def end_kernel(plan, held, last_ref, grad_ref, out_ref, kernel_ref, edges):
    c, bx, by, s = plan.channels, plan.bx, plan.by, plan.devices
    edges[...] = last_ref[:, plan.rows :, :].astype(F32).reshape(edges.shape)
    count = 9 * c // (2 * s)
    for t in range(count):
        rows = edges[pl.ds(t, s, stride=EDGE), :]
        for h in range(2):
            start = (h * count + t) * s
            tap, first = start // c, start % c
            a, b = 2 - tap // 3, 2 - tap % 3
            kernel_ref[a, b, first : first + s, :] = rows[:, h * c : (h + 1) * c]
    syn = last_ref[:, : plan.rows, :].astype(F32).reshape(c, bx, by)
    out_ref[...] = (grad_ref[...] + syn).astype(BF16)


def fast_body(plan, field, spectral_weight, kernel_weight, cotangent):
    channels, bx, by, n, cpd = plan.channels, plan.bx, plan.by, plan.devices, plan.cpd
    anywhere = pl.BlockSpec(memory_space=pl.ANY)
    here = pl.BlockSpec(memory_space=pltpu.VMEM)

    def exchange(x):
        return lax.all_to_all(x, BOTH, 0, 0, tiled=True)

    def rows_of(count):
        return jax.ShapeDtypeStruct((n, count, by), BF16)

    def call(
        kernel, outs, *args, us=1.0, scratch=(), mib=56, raw=(), use=(), after=(), spec=None,
        alias=False,
    ):
        several = isinstance(outs, tuple)
        outs = outs if several else (outs,)
        steps = (len(raw), len(args), len(use), len(after))

        def run(*refs):
            groups = []
            for step in steps:
                groups.append(refs[:step])
                refs = refs[step:]
            kernel(plan, dict(zip(use, groups[2])), *groups[0], *groups[1], *refs)

        results = pl.pallas_call(
            run,
            out_shape=outs,
            in_specs=[anywhere] * len(raw)
            + [here] * (len(args) + len(use))
            + [anywhere] * len(after),
            out_specs=(spec or here,) * len(outs),
            scratch_shapes=scratch,
            input_output_aliases={sum(steps) - 1: 0} if alias else {},
            cost_estimate=pl.CostEstimate(
                flops=int(us * 1.0e9), bytes_accessed=1024, transcendentals=0
            ),
            compiler_params=pltpu.CompilerParams(vmem_limit_bytes=mib * 1024 * 1024),
        )(*raw, *args, *(held[name] for name in use), *after)
        return results if several else results[0]

    flat = pltpu.VMEM((n * plan.mx, plan.lanes), F32)
    turned = pltpu.VMEM((plan.mx, channels, 2 * plan.my), F32)
    rows = pltpu.VMEM((plan.mx, 2 * plan.my, channels), F32)
    block = pltpu.VMEM((channels * bx, by), F32)
    edges = pltpu.VMEM((n * EDGE, by), F32)
    paired = pltpu.VMEM((channels, by), F32)
    taps = pltpu.VMEM((3 * channels, (bx + 2) * by), BF16)
    place = pltpu.VMEM(field.shape, BF16)
    kernel_place = pltpu.VMEM(kernel_weight.shape, BF16)
    field_flat = pltpu.VMEM((channels, bx * by), BF16)
    modes_scratch = [
        flat,
        turned,
        rows,
        pltpu.VMEM((plan.mx, plan.my, channels, 2 * channels), BF16),
        pltpu.SemaphoreType.DMA((plan.mx // CHUNK,)),
    ]
    edge_tables = ("pick_rows", "pick_cols", "window")

    field_c = exchange(field.reshape(n, plan.rows, by))
    sources = {name: jnp.asarray(t) for name, t in plan.named().items()}
    packed_shape = (plan.mx, plan.my, channels, 2 * channels)
    half = plan.mx // 2
    chunk_sems = pltpu.SemaphoreType.DMA((half // CHUNK,))
    pack_scratch = [
        pltpu.VMEM((2, half) + packed_shape[1:-1] + (channels,), BF16),
        pltpu.VMEM((half,) + packed_shape[1:], BF16),
    ]
    weights, *held = pl.pallas_call(
        partial(load_kernel, plan, half),
        out_shape=(jax.ShapeDtypeStruct(packed_shape, BF16),)
        + tuple(pltpu.VMEM(t.shape, t.dtype) for t in sources.values()),
        in_specs=[anywhere] * (1 + len(sources)),
        out_specs=(anywhere,) + (here,) * len(sources),
        scratch_shapes=pack_scratch
        + [pltpu.SemaphoreType.DMA((len(sources),)), chunk_sems, chunk_sems],
        cost_estimate=pl.CostEstimate(flops=5_000_000_000, bytes_accessed=1024, transcendentals=0),
        compiler_params=pltpu.CompilerParams(vmem_limit_bytes=58 * 1024 * 1024),
    )(spectral_weight, *sources.values())
    held = dict(zip(sources, held))
    a_part = call(
        first_kernel,
        rows_of(plan.mx + EDGE),
        field_c,
        use=("col", "row") + edge_tables,
        mib=20,
    )
    a_both = exchange(a_part)
    weights = call(
        lambda plan, held, r_ref, after_ref, first_ref, *refs: pack_rows(
            plan, half, half, r_ref, *refs
        ),
        jax.ShapeDtypeStruct(packed_shape, BF16),
        raw=(spectral_weight, a_part, weights),
        scratch=pack_scratch + [chunk_sems, chunk_sems],
        spec=anywhere,
        us=5.0,
        alias=True,
    )
    b_part = call(
        mix_kernel,
        rows_of(plan.mx + 2 * plan.rows),
        a_both,
        raw=(weights, field, cotangent.reshape(n, plan.rows, by), kernel_weight),
        scratch=[place, kernel_place, pltpu.SemaphoreType.DMA((2,))]
        + [block, edges, paired, taps]
        + modes_scratch
        + [pltpu.SemaphoreType.DMA],
        us=6.0,
    )
    g_part = call(
        middle_kernel,
        rows_of(plan.mx + plan.rows + EDGE),
        exchange(b_part),
        use=("row_s", "col", "row") + edge_tables,
        mib=20,
        scratch=[pltpu.VMEM((plan.nx, cpd * plan.ny), BF16)],
        us=2.6,
    )
    g_both = exchange(g_part)
    layer_out, grad_sum, back_terms = call(
        back_kernel,
        (
            jax.ShapeDtypeStruct(field.shape, BF16),
            jax.ShapeDtypeStruct(field.shape, F32),
            rows_of(plan.mx + EDGE),
        ),
        g_both,
        raw=(weights, field, cotangent, kernel_weight),
        scratch=[place, place, kernel_place, pltpu.SemaphoreType.DMA((3,))]
        + [block, edges, paired, taps, field_flat]
        + modes_scratch,
        us=8.0,
    )
    back_both = exchange(back_terms)

    def outer_part(first_j, count, after, alias):
        return call(
            lambda plan, *refs: outer_kernel(plan, first_j, count, *refs),
            jax.ShapeDtypeStruct(spectral_weight.shape, BF16),
            a_both,
            g_both,
            scratch=[
                flat,
                flat,
                turned,
                turned,
                pltpu.VMEM((2, count, plan.my, channels, channels), BF16),
                pltpu.SemaphoreType.DMA((count // CHUNK,)),
            ],
            spec=anywhere,
            us=6.4,
            after=after,
            alias=alias,
        )

    spectral_half = outer_part(0, half, (back_terms,), False)
    last_part = call(
        last_kernel,
        rows_of(plan.rows + EDGE),
        back_both,
        use=("row_s", "col"),
        us=1.3,
        mib=44,
        after=(spectral_half,),
    )
    last_both = exchange(last_part)
    spectral_grad = outer_part(half, half, (last_part, spectral_half), True)
    field_grad, kernel_grad = call(
        end_kernel,
        (
            jax.ShapeDtypeStruct(field.shape, BF16),
            jax.ShapeDtypeStruct((3, 3, channels, channels), F32),
        ),
        last_both,
        grad_sum,
        scratch=[edges],
        mib=20,
    )
    return (layer_out, field_grad, spectral_grad, kernel_grad)


def body(field, spectral_weight, kernel_weight, cotangent):
    plan = Plan(*field.shape, lax.axis_size("gx"), lax.axis_size("gy"))
    if plan.fits:
        return fast_body(plan, field, spectral_weight, kernel_weight, cotangent)
    return general_body(field, spectral_weight, kernel_weight, cotangent)


def solution(mesh):
    in_specs = (P(None, "gx", "gy"), P(None, "gx", "gy", None, None), P(), P(None, "gx", "gy"))
    out_specs = (P(None, "gx", "gy"), P(None, "gx", "gy"), P(None, "gx", "gy", None, None), P())
    return jax.shard_map(body, mesh=mesh, in_specs=in_specs, out_specs=out_specs, check_vma=False)
```

```python
from functools import partial
import math

import jax
import jax.numpy as jnp
import ml_dtypes
import numpy as np
from jax import lax
from jax.experimental import pallas as pl
from jax.experimental.pallas import tpu as pltpu
from jax.sharding import PartitionSpec as P

KX = 128
KY = 128


def extended(array, sides, width):
    for axis, dim in sides:
        count, length = (lax.axis_size(axis), array.shape[dim])
        up = [(i, (i + 1) % count) for i in range(count)]
        down = [(j, i) for i, j in up]
        last = lax.slice_in_dim(array, length - width, length, axis=dim)
        initial = lax.slice_in_dim(array, 0, width, axis=dim)
        before = lax.ppermute(last, axis, up)
        after = lax.ppermute(initial, axis, down)
        array = jnp.concatenate([before, array, after], axis=dim)
    return array


def phases(waves, points, length):
    wrapped = jnp.mod(waves[:, None] * points[None, :], length).astype(jnp.float32)
    return wrapped * (2.0 * math.pi / length)


def widen(field):
    return extended(field, (("gx", 1), ("gy", 2)), 1)


def general_body(field, spectral_weight, kernel_weight, cotangent):
    highest = lax.Precision.HIGHEST
    channels, block_rows, block_cols = field.shape
    rows_total = block_rows * lax.axis_size("gx")
    cols_total = block_cols * lax.axis_size("gy")
    scale = 1.0 / math.sqrt(rows_total * cols_total)
    row_coord = lax.axis_index("gx") * block_rows + jnp.arange(block_rows, dtype=jnp.int32)
    col_coord = lax.axis_index("gy") * block_cols + jnp.arange(block_cols, dtype=jnp.int32)
    modes_x = KX // lax.axis_size("gx")
    modes_y = KY // lax.axis_size("gy")

    def analyse(source):
        waves = jnp.arange(lax.axis_size("gy") * modes_y, dtype=jnp.int32)
        angles = phases(waves, col_coord, cols_total)
        table = jnp.concatenate([jnp.cos(angles), -jnp.sin(angles)], 0).astype(jnp.bfloat16)
        product = jnp.dot(
            source.reshape(channels * block_rows, block_cols),
            table.T,
            preferred_element_type=jnp.float32,
        )
        product = product.reshape(channels, block_rows, 2, lax.axis_size("gy") * modes_y).transpose(
            3, 1, 2, 0
        )
        col_modes = lax.psum_scatter(
            product.reshape(lax.axis_size("gy") * modes_y, block_rows, 2 * channels),
            "gy",
            scatter_dimension=0,
            tiled=True,
        )
        split_modes = col_modes.reshape(modes_y, block_rows, 2, channels)
        real_in = split_modes[:, :, 0]
        imag_in = split_modes[:, :, 1]
        waves = jnp.arange(lax.axis_size("gx") * modes_x, dtype=jnp.int32) - KX // 2
        angles = phases(waves, row_coord, rows_total)
        cosines = jnp.cos(angles)
        sines = jnp.sin(angles)
        contract = partial(jnp.einsum, "jx,lxc->jlc", precision=highest)
        real_out = contract(cosines, real_in) + contract(sines, imag_in)
        imag_out = contract(cosines, imag_in) - contract(sines, real_in)
        return lax.psum_scatter(
            jnp.stack([real_out, imag_out], 2).reshape(
                lax.axis_size("gx") * modes_x, modes_y, 2 * channels
            )
            * scale,
            "gx",
            scatter_dimension=0,
            tiled=True,
        ).reshape(modes_x, modes_y, 2, channels)

    def synthesise(modes):
        start_rows = jnp.zeros((modes_y, block_rows, 2 * channels), jnp.float32)
        shard_rows = lax.all_gather(
            modes.reshape(modes_x, modes_y, 2 * channels), "gx", axis=0, tiled=True
        )
        amount = shard_rows.shape[0]
        waves = jnp.arange(amount, dtype=jnp.int32) - KX // 2
        angles = phases(waves, row_coord, rows_total)
        cosines = jnp.cos(angles).astype(jnp.bfloat16)
        sines = jnp.sin(angles).astype(jnp.bfloat16)
        split_rows = shard_rows.reshape(amount, modes_y, 2, channels)
        real_in = split_rows[:, :, 0]
        imag_in = split_rows[:, :, 1]
        contract = partial(jnp.einsum, "jx,jlc->lxc", preferred_element_type=jnp.float32)
        real_out = contract(cosines, real_in) - contract(sines, imag_in)
        imag_out = contract(sines, real_in) + contract(cosines, imag_in)
        row_sum = start_rows + jnp.stack([real_out, imag_out], 2).reshape(
            modes_y, block_rows, 2 * channels
        )
        row_sum = row_sum.astype(jnp.bfloat16)
        shard_rows = lax.all_gather(row_sum, "gy", axis=0, tiled=True)
        amount = shard_rows.shape[0]
        waves = jnp.arange(amount, dtype=jnp.int32)
        angles = phases(waves, col_coord, cols_total)
        table = jnp.stack([jnp.cos(angles), -jnp.sin(angles)], 1).astype(jnp.bfloat16)
        split_rows = shard_rows.reshape(amount, block_rows, 2, channels)
        return (
            jnp.einsum("lxpc,lpy->cxy", split_rows, table, preferred_element_type=jnp.float32)
            * scale
        )

    padded_field = widen(field)
    hidden = jnp.zeros((channels, block_rows, block_cols), jnp.float32)
    for row_tap in range(3):
        for col_tap in range(3):
            window = padded_field[:, row_tap : row_tap + block_rows, col_tap : col_tap + block_cols]
            hidden = hidden + jnp.einsum(
                "oi,ixy->oxy",
                kernel_weight[row_tap, col_tap],
                window,
                preferred_element_type=jnp.float32,
            )
    amodes = analyse(field)
    areal = amodes[:, :, 0]
    aimag = amodes[:, :, 1]
    wreal = spectral_weight[0].astype(jnp.float32)
    wimag = spectral_weight[1].astype(jnp.float32)
    mixing = partial(jnp.einsum, "jli,jlio->jlo", precision=highest)
    breal = mixing(areal, wreal) - mixing(aimag, wimag)
    bimag = mixing(areal, wimag) + mixing(aimag, wreal)
    wave_index = lax.axis_index("gy") * modes_y + jnp.arange(modes_y, dtype=jnp.int32)
    weights = jnp.where(wave_index == 0, 1.0, 2.0).astype(jnp.float32)[None, :, None, None]
    bmodes = (jnp.stack([breal, bimag], 2) * weights).astype(jnp.bfloat16)
    hidden = hidden + synthesise(bmodes)
    activated, pullback = jax.vjp(jax.nn.gelu, hidden)
    layer_out = (field.astype(jnp.float32) + activated).astype(jnp.bfloat16)
    grads = pullback(cotangent.astype(jnp.float32))[0].astype(jnp.bfloat16)
    gmodes = analyse(grads) * weights
    greal = gmodes[:, :, 0]
    gimag = gmodes[:, :, 1]
    outer = partial(jnp.einsum, "jli,jlo->jlio", precision=highest)
    spectral_grad = jnp.stack(
        [outer(areal, greal) + outer(aimag, gimag), outer(areal, gimag) - outer(aimag, greal)], 0
    ).astype(jnp.bfloat16)
    back = partial(jnp.einsum, "jlio,jlo->jli", precision=highest)
    back_real = back(wreal, greal) + back(wimag, gimag)
    back_imag = back(wreal, gimag) - back(wimag, greal)
    back_modes = jnp.stack([back_real, back_imag], 2).astype(jnp.bfloat16)
    padded_grads = widen(grads)
    adjoint = jnp.zeros((channels, block_rows, block_cols), jnp.float32)
    tap_rows = []
    for row_tap in range(3):
        tap_cols = []
        for col_tap in range(3):
            window = padded_grads[
                :, 2 - row_tap : 2 - row_tap + block_rows, 2 - col_tap : 2 - col_tap + block_cols
            ]
            adjoint = adjoint + jnp.einsum(
                "oi,oxy->ixy",
                kernel_weight[row_tap, col_tap],
                window,
                preferred_element_type=jnp.float32,
            )
            source_window = padded_field[
                :, row_tap : row_tap + block_rows, col_tap : col_tap + block_cols
            ]
            tap_cols.append(
                jnp.einsum("oxy,ixy->oi", grads, source_window, preferred_element_type=jnp.float32)
            )
        tap_rows.append(jnp.stack(tap_cols, 0))
    kernel_grad = lax.psum(jnp.stack(tap_rows, 0), ("gx", "gy"))
    field_grad = (cotangent.astype(jnp.float32) + adjoint + synthesise(back_modes)).astype(
        jnp.bfloat16
    )
    return (layer_out, field_grad, spectral_grad, kernel_grad)


BF16 = jnp.bfloat16
F32 = jnp.float32
BOTH = ("gx", "gy")
EDGE = 16
GROUP = 8
CHUNK = 2
MIXED = 8


class Plan:
    def __init__(self, channels, block_rows, block_cols, gx, gy):
        self.gx, self.gy, self.devices = gx, gy, gx * gy
        self.channels, self.bx, self.by = channels, block_rows, block_cols
        self.nx, self.ny = block_rows * gx, block_cols * gy
        self.mx, self.my = KX // gx, KY // gy
        self.cpd = channels // self.devices if channels % self.devices == 0 else 0
        self.lanes = self.cpd * 2 * self.my
        self.rows = self.cpd * self.bx
        self.fits = (
            self.cpd == 2
            and channels == 64
            and self.lanes == 128
            and self.by == 128
            and self.bx == 16
            and KX % gx == 0
            and KY % gy == 0
            and self.mx == 16
            and self.my % GROUP == 0
            and gy % 2 == 0
            and KX == 128
            and self.nx == 128
        )
        self.scale = 1.0 / math.sqrt(self.nx * self.ny)

    def tables(self):
        two_pi = np.float32(2.0 * math.pi)
        waves, points = np.arange(KY), np.arange(self.ny)
        angles = np.float32((waves[:, None] * points[None, :]) % self.ny) * (two_pi / self.ny)
        cos, sin = np.cos(angles).T, np.sin(angles).T
        split = (self.ny, self.gy, self.my)
        cos, sin = cos.reshape(split), sin.reshape(split)
        top, bottom = np.stack([cos, -sin], 2), np.stack([-sin, -cos], 2)
        col = np.stack([top, bottom], 1).reshape(self.ny, -1).astype(ml_dtypes.bfloat16)
        rows = np.arange(KX) - KX // 2
        points = np.arange(self.nx)
        angles = np.float32((rows[:, None] * points[None, :]) % self.nx) * (two_pi / self.nx)
        row = np.concatenate([np.cos(angles), np.sin(angles)], 1).astype(np.float32)
        high = row.astype(ml_dtypes.bfloat16)
        low = (row - high.astype(np.float32)).astype(ml_dtypes.bfloat16)
        row_analysis = np.concatenate([high, low], 1)
        row_synthesis = np.concatenate([np.cos(angles).T, np.sin(angles).T], 0)
        row_synthesis = row_synthesis.astype(ml_dtypes.bfloat16)
        return col, row_analysis, row_synthesis

    def named(self):
        names = ("col", "row", "row_s", "pick_rows", "pick_cols", "window")
        return dict(zip(names, self.tables() + self.pickers()))

    def pickers(self):
        pick_rows = np.zeros((self.gx, EDGE, self.cpd, self.nx), np.float32)
        pick_cols = np.zeros((self.gy, EDGE, self.cpd, self.ny), np.float32)
        window = np.zeros((self.nx, self.gx, self.by), np.float32)
        for c in range(self.cpd):
            for g in range(self.gx):
                pick_rows[g, 2 * c, c, (g * self.bx - 1) % self.nx] = 1
                pick_rows[g, 2 * c + 1, c, ((g + 1) * self.bx) % self.nx] = 1
            for g in range(self.gy):
                pick_cols[g, 2 * self.cpd + 2 * c, c, (g * self.by - 1) % self.ny] = 1
                pick_cols[g, 2 * self.cpd + 2 * c + 1, c, ((g + 1) * self.by) % self.ny] = 1
        for g in range(self.gx):
            for t in range(self.bx + 2):
                window[(g * self.bx - 1 + t) % self.nx, g, t] = 1
        kind = ml_dtypes.bfloat16
        return (
            pick_rows.reshape(self.gx * EDGE, -1).astype(kind),
            pick_cols.reshape(self.gy * EDGE, -1).astype(kind),
            window.reshape(self.nx, -1).astype(kind),
        )


def dot(a, b):
    return jnp.dot(a, b, preferred_element_type=F32)


def dot_nt(a, b):
    return lax.dot_general(a, b, (((1,), (1,)), ((), ())), preferred_element_type=F32)


def interleave(plan, parts):
    half = plan.lanes // 2
    lane = lax.broadcasted_iota(jnp.int32, (1, plan.lanes), 1)
    tiles = []
    for k in range(plan.gy // 2):
        first, second = (p[:, k * plan.lanes : (k + 1) * plan.lanes] for p in parts)
        tiles.append(jnp.where(lane < half, first, pltpu.roll(second, half, 1)))
        tiles.append(jnp.where(lane < half, pltpu.roll(first, half, 1), second))
    return jnp.concatenate(tiles, 1)


def separate(plan, values):
    half = plan.lanes // 2
    lane = lax.broadcasted_iota(jnp.int32, (1, plan.lanes), 1)
    parts = ([], [])
    for k in range(plan.gy // 2):
        even = values[:, 2 * k * plan.lanes : (2 * k + 1) * plan.lanes]
        odd = values[:, (2 * k + 1) * plan.lanes : (2 * k + 2) * plan.lanes]
        parts[0].append(jnp.where(lane < half, even, pltpu.roll(odd, half, 1)))
        parts[1].append(jnp.where(lane < half, pltpu.roll(even, half, 1), odd))
    return [jnp.concatenate(p, 1) for p in parts]


def analyse_plane(plan, held, planes, weight, out_ref):
    col = held["col"]
    half = col.shape[1] // 2
    along_y = [
        dot(planes[:, c * plan.ny : (c + 1) * plan.ny], col[...]) for c in range(plan.cpd)
    ]
    stacked = jnp.concatenate(
        [
            interleave(plan, [p[:, :half] for p in along_y]),
            interleave(plan, [p[:, half:] for p in along_y]),
        ],
        0,
    ).astype(BF16)
    modes = dot(held["row"][...], jnp.concatenate([stacked, stacked], 0)) * weight
    modes = modes.astype(BF16)
    for i in range(plan.gx):
        for k in range(plan.gy):
            out_ref[i * plan.gy + k, : plan.mx] = modes[
                i * plan.mx : (i + 1) * plan.mx, k * plan.lanes : (k + 1) * plan.lanes
            ]


def put_edges(plan, held, planes, out_ref, start):
    stacked = jnp.concatenate(
        [planes[:, c * plan.ny : (c + 1) * plan.ny] for c in range(plan.cpd)], 0
    )
    edge_rows = dot(held["pick_rows"][...], stacked)
    picked = dot_nt(held["pick_cols"][...], planes).astype(BF16)
    edge_cols = dot(picked, held["window"][...])
    for i in range(plan.gx):
        for k in range(plan.gy):
            tile = (
                edge_rows[i * EDGE : (i + 1) * EDGE, k * plan.by : (k + 1) * plan.by]
                + edge_cols[k * EDGE : (k + 1) * EDGE, i * plan.by : (i + 1) * plan.by]
            )
            out_ref[i * plan.gy + k, start : start + EDGE] = tile.astype(BF16)


def synthesise_plane(plan, held, modes_ref, weight):
    columns = []
    for k in range(plan.gy):
        columns.append(
            jnp.concatenate([modes_ref[i * plan.gy + k, : plan.mx] for i in range(plan.gx)], 0)
        )
    sums = dot(held["row_s"][...], jnp.concatenate(columns, 1))
    if weight is not None:
        sums = sums * weight
    top, bottom = separate(plan, sums[: plan.nx]), separate(plan, sums[plan.nx :])
    planes = []
    for c in range(plan.cpd):
        left = jnp.concatenate([top[c], bottom[c]], 1).astype(BF16)
        planes.append(dot_nt(left, held["col"][...]))
    return jnp.concatenate(planes, 1)


def read_plane(plan, ref, c, k, first=0):
    rows = slice(first + c * plan.bx, first + (c + 1) * plan.bx)
    return jnp.concatenate([ref[i * plan.gy + k, rows] for i in range(plan.gx)], 0)


def write_plane(plan, ref, c, k, values, first=0):
    rows = slice(first + c * plan.bx, first + (c + 1) * plan.bx)
    for i in range(plan.gx):
        ref[i * plan.gy + k, rows] = values[i * plan.bx : (i + 1) * plan.bx]


def first_kernel(plan, held, field_ref, out_ref):
    planes = jnp.concatenate(
        [read_plane(plan, field_ref, c, k) for c in range(plan.cpd) for k in range(plan.gy)], 1
    )
    analyse_plane(plan, held, planes, plan.scale, out_ref)
    put_edges(plan, held, planes, out_ref, plan.mx)


def gelu_parts(z):
    factor = math.sqrt(2.0 / math.pi)
    tanh = jnp.tanh(factor * (z + 0.044715 * (z * z * z)))
    cdf = 0.5 * (1.0 + tanh)
    slope = cdf + 0.5 * z * (1.0 - tanh * tanh) * (factor * (1.0 + (3.0 * 0.044715) * (z * z)))
    return z * cdf, slope


def middle_kernel(plan, held, modes_ref, out_ref, grads):
    lane = lax.broadcasted_iota(jnp.int32, (1, plan.gy * plan.lanes), 1)
    zero = jnp.logical_and(lane < plan.lanes, lax.rem(lane, plan.my) == 0)
    doubled = jnp.where(zero, 1.0, 2.0)
    syn = synthesise_plane(plan, held, modes_ref, doubled) * plan.scale
    for c in range(plan.cpd):
        for k in range(plan.gy):
            start = c * plan.ny + k * plan.by
            z = syn[:, start : start + plan.by] + read_plane(plan, modes_ref, c, k, plan.mx).astype(F32)
            z = z.astype(BF16)
            write_plane(plan, out_ref, c, k, z, plan.mx)
            slope = gelu_parts(z.astype(F32))[1]
            cot = read_plane(plan, modes_ref, plan.cpd + c, k, plan.mx).astype(F32)
            grads[:, start : start + plan.by] = (cot * slope).astype(BF16)
    planes = grads[...]
    analyse_plane(plan, held, planes, doubled * plan.scale, out_ref)
    put_edges(plan, held, planes, out_ref, plan.mx + plan.rows)


def last_kernel(plan, held, both_ref, out_ref):
    syn = synthesise_plane(plan, held, both_ref, None) * plan.scale
    syn = syn.astype(BF16)
    for c in range(plan.cpd):
        for k in range(plan.gy):
            start = c * plan.ny + k * plan.by
            write_plane(plan, out_ref, c, k, syn[:, start : start + plan.by])
    terms = both_ref[0, plan.mx :].astype(F32)
    for s in range(1, plan.devices):
        terms = terms + both_ref[s, plan.mx :].astype(F32)
    terms = terms.astype(BF16)
    for s in range(plan.devices):
        out_ref[s, plan.rows :] = terms


def gather_modes(plan, x_ref, flat, turned, j):
    s, half = plan.devices, plan.lanes // 2
    values = flat[pl.ds(j, s, stride=plan.mx), :]
    for c in range(plan.cpd):
        turned[j, pl.ds(c, s, stride=plan.cpd), :] = values[:, c * half : (c + 1) * half]


def spread(plan, x_ref, flat):
    flat[...] = x_ref[:, : plan.mx, :].astype(F32).reshape(plan.devices * plan.mx, plan.lanes)


def modes_to_rows(plan, x_ref, flat, turned, rows):
    spread(plan, x_ref, flat)
    for j in range(plan.mx):
        gather_modes(plan, x_ref, flat, turned, j)
        rows[j] = turned[j].T


def rows_to_modes(plan, values, turned, flat, j):
    s = plan.devices
    turned[j] = values.T
    parts = [turned[j, pl.ds(c, s, stride=plan.cpd), :] for c in range(plan.cpd)]
    flat[pl.ds(j, s, stride=plan.mx), :] = jnp.concatenate(parts, 1)


def group_mask(rows, groups, width):
    row = lax.broadcasted_iota(jnp.int32, (rows, groups * width), 0)
    lane = lax.broadcasted_iota(jnp.int32, (rows, groups * width), 1)
    return lax.rem(row, groups) == lax.div(lane, width)


def pack_rows(plan, first_j, count, r_ref, packed_ref, arrived, packed, in_sems, out_sems, others=()):
    chunks = count // CHUNK

    def part(t, start=0):
        return pl.ds(start + t * CHUNK, CHUNK)

    loads = [
        pltpu.make_async_copy(r_ref.at[:, part(t, first_j)], arrived.at[:, part(t)], in_sems.at[t])
        for t in range(chunks)
    ]
    stores = [
        pltpu.make_async_copy(packed.at[part(t)], packed_ref.at[part(t, first_j)], out_sems.at[t])
        for t in range(chunks)
    ]
    for copy in loads + list(others):
        copy.start()
    for t in range(chunks):
        loads[t].wait()
        for j in range(t * CHUNK, (t + 1) * CHUNK):
            packed[j] = jnp.concatenate([arrived[0, j], arrived[1, j]], -1)
        stores[t].start()
    for copy in list(others) + stores:
        copy.wait()


def load_kernel(plan, half, *refs):
    count = (len(refs) - 7) // 2
    r_ref, sources = refs[0], refs[1 : 1 + count]
    packed_ref, places = refs[1 + count], refs[2 + count : 2 + 2 * count]
    arrived, packed, sems, in_sems, out_sems = refs[2 + 2 * count :]
    copies = [
        pltpu.make_async_copy(source, place, sems.at[i])
        for i, (source, place) in enumerate(zip(sources, places))
    ]
    pack_rows(plan, 0, half, r_ref, packed_ref, arrived, packed, in_sems, out_sems, copies)


def each_mode_row(plan, product, first, mixed, r_ref, x_ref, y_ref, flat, turned, rows, held, sems):
    width = plan.channels
    copies = [
        pltpu.make_async_copy(
            r_ref.at[pl.ds(t * mixed, mixed)], held.at[pl.ds(t * mixed, mixed)], sems.at[t]
        )
        for t in range(plan.mx // mixed)
    ]
    for copy in copies:
        copy.start()
    modes_to_rows(plan, x_ref, flat, turned, rows)
    first()
    mask = group_mask(2 * GROUP, GROUP, width)

    def step(j, carry):
        real_out, imag_out = [], []
        for g in range(plan.my // GROUP):
            start = g * GROUP
            real = rows[j, start : start + GROUP, :]
            imag = rows[j, plan.my + start : plan.my + start + GROUP, :]
            weights = held[j, start : start + GROUP].reshape(GROUP * width, 2 * width)
            real, imag = product(mask, real, imag, weights)
            real_out.append(real)
            imag_out.append(imag)
        rows_to_modes(plan, jnp.concatenate(real_out + imag_out, 0), turned, flat, j)
        return carry

    for t, copy in enumerate(copies):
        copy.wait()
        lax.fori_loop(t * mixed, (t + 1) * mixed, step, 0, unroll=16 if mixed == 16 else 8)
    values = flat[...].reshape(plan.devices, plan.mx, plan.lanes)
    y_ref[:, : plan.mx] = values.astype(BF16)


class Arrival:
    def __init__(self, source, place, sem):
        self.copy, self.place, self.there = pltpu.make_async_copy(source, place, sem), place, False
        self.copy.start()

    def __getitem__(self, index):
        if not self.there:
            self.copy.wait()
            self.there = True
        return self.place[index]


def bring(sources, refs):
    count = len(sources)
    arrivals = {
        name: Arrival(source, refs[i], refs[count].at[i])
        for i, (name, source) in enumerate(sources)
    }
    return arrivals, refs[count + 1 :]


def mix_kernel(plan, held, r_ref, field_ref, cot_ref, kernel_ref, x_ref, y_ref, kept_ref, *refs):
    kept_ref[...] = x_ref[:, : plan.mx]
    width = plan.channels
    held, refs = bring((("field", field_ref), ("kernel", kernel_ref)), refs)
    cot = pltpu.make_async_copy(cot_ref, y_ref.at[:, pl.ds(plan.mx + plan.rows, plan.rows)], refs[-1])
    cot.start()
    refs = refs[:-1]

    def product(mask, real, imag, weights):
        left = jnp.concatenate([jnp.concatenate([real, imag], 0)] * GROUP, 1)
        mixed = dot(jnp.where(mask, left, 0.0).astype(BF16), weights)
        return (
            mixed[:GROUP, :width] - mixed[GROUP:, width:],
            mixed[:GROUP, width:] + mixed[GROUP:, :width],
        )

    conv = partial(conv_part, plan, held, x_ref, y_ref, *refs[:4])
    each_mode_row(plan, product, conv, MIXED, r_ref, x_ref, y_ref, *refs[4:])
    cot.wait()


def back_kernel(
    plan, held, r_ref, field_ref, cot_ref, kernel_ref, g_ref, layer_ref, grad_ref, both_ref,
    kept_ref, *refs
):
    kept_ref[...] = g_ref[:, : plan.mx]
    width = plan.channels
    sources = (("field", field_ref), ("cotangent", cot_ref), ("kernel", kernel_ref))
    held, refs = bring(sources, refs)

    def product(mask, real, imag, weights):
        left = jnp.concatenate(
            [jnp.concatenate([real, imag], 1), jnp.concatenate([imag, -real], 1)], 0
        )
        mixed = jnp.where(mask, dot_nt(left.astype(BF16), weights), 0.0)
        total = mixed[:, : 2 * width]
        for i in range(1, GROUP // 2):
            total = total + mixed[:, 2 * i * width : 2 * (i + 1) * width]
        total = total[:, :width] + total[:, width:]
        return total[:GROUP], total[GROUP:]

    space = partial(space_part, plan, held, g_ref, layer_ref, grad_ref, both_ref, *refs[:5])
    each_mode_row(plan, product, space, plan.mx, r_ref, g_ref, both_ref, *refs[5:])


def outer_kernel(
    plan, first_j, count, held, x_ref, g_ref, *refs
):
    out_ref, x_flat, g_flat, a_turned, g_turned, slots, sems = refs
    my, width = plan.my, plan.channels
    spread(plan, x_ref, x_flat)
    spread(plan, g_ref, g_flat)
    for j in range(first_j, first_j + count):
        gather_modes(plan, x_ref, x_flat, a_turned, j)
        gather_modes(plan, g_ref, g_flat, g_turned, j)
    lane = lax.rem(lax.broadcasted_iota(jnp.int32, (width, 2 * my), 1), my)
    copies = []
    for j in range(first_j, first_j + count):
        left = a_turned[j]
        g_rows = g_turned[j].T
        g_real, g_imag = g_rows[:my], g_rows[my:]
        right = jnp.concatenate(
            [jnp.concatenate([g_real, g_imag], 1), jnp.concatenate([g_imag, -g_real], 1)], 0
        ).astype(BF16)
        for g in range(my // GROUP):
            picked = jnp.concatenate(
                [jnp.where(lane == g * GROUP + l, left, 0.0) for l in range(GROUP)], 0
            ).astype(BF16)
            value = dot(picked, right).astype(BF16)
            for part in range(2):
                slots[part, j - first_j, g * GROUP : (g + 1) * GROUP] = value[
                    :, part * width : (part + 1) * width
                ].reshape(GROUP, width, width)
        if (j + 1) % CHUNK == 0:
            t = (j + 1 - first_j) // CHUNK - 1
            copies.append(
                pltpu.make_async_copy(
                    slots.at[:, pl.ds(t * CHUNK, CHUNK)],
                    out_ref.at[:, pl.ds(first_j + t * CHUNK, CHUNK)],
                    sems.at[t],
                )
            )
            copies[-1].start()
    for copy in copies:
        copy.wait()


def fill_taps(plan, block, edges, paired, taps):
    c, bx, by, s = plan.channels, plan.bx, plan.by, plan.devices

    def edge(first):
        for p in range(plan.cpd):
            paired[pl.ds(p, s, stride=plan.cpd), :] = edges[
                pl.ds(first + 2 * p, s, stride=EDGE), :
            ]
        return paired[...]

    top, bottom = edge(0), edge(1)
    left, right = edge(2 * plan.cpd), edge(2 * plan.cpd + 1)
    lane = lax.broadcasted_iota(jnp.int32, (c, by), 1)
    for x in range(bx + 2):
        if x == 0:
            row = top
        elif x == bx + 1:
            row = bottom
        else:
            row = block[pl.ds(x - 1, c, stride=bx), :]
        lanes = slice(x * by, (x + 1) * by)
        taps[:c, lanes] = jnp.where(
            lane == 0, left[:, x : x + 1], pltpu.roll(row, 1, 1)
        ).astype(BF16)
        taps[c : 2 * c, lanes] = row.astype(BF16)
        taps[2 * c :, lanes] = jnp.where(
            lane == by - 1, right[:, x : x + 1], pltpu.roll(row, by - 1, 1)
        ).astype(BF16)


def convolve(plan, weights, taps, out):
    bx, by = plan.bx, plan.by
    total = dot(weights[0], taps[:, : bx * by])
    for a in range(1, 3):
        total = total + dot(weights[a], taps[:, a * by : (a + bx) * by])
    for x in range(bx):
        out[pl.ds(x, plan.channels, stride=bx), :] = total[:, x * by : (x + 1) * by]


def conv_part(plan, held, both_ref, out_ref, block, edges, paired, taps):
    edges[...] = both_ref[:, plan.mx :, :].astype(F32).reshape(edges.shape)
    block[...] = held["field"][...].astype(F32).reshape(block.shape)
    fill_taps(plan, block, edges, paired, taps)
    kernel_ref = held["kernel"]
    weights = [jnp.concatenate([kernel_ref[a, b] for b in range(3)], 1) for a in range(3)]
    convolve(plan, weights, taps, block)
    shape = (plan.devices, plan.rows, plan.by)
    out_ref[:, plan.mx : plan.mx + plan.rows] = block[...].reshape(shape).astype(BF16)


def space_part(
    plan, held, z_ref, layer_ref, grad_ref, both_ref, block, edges, paired, taps, flat
):
    c, bx, by, s = plan.channels, plan.bx, plan.by, plan.devices
    z = z_ref[:, plan.mx : plan.mx + plan.rows, :].astype(F32).reshape(c, bx, by)
    activated, slope = gelu_parts(z)
    field = held["field"][...].astype(F32)
    layer_ref[...] = (field + activated).astype(BF16)
    block[...] = field.reshape(block.shape)
    for x in range(bx):
        flat[:, x * by : (x + 1) * by] = block[pl.ds(x, c, stride=bx), :].astype(BF16)
    cot_ref = held["cotangent"]
    grads = (cot_ref[...].astype(F32) * slope).astype(BF16).astype(F32)
    block[...] = grads.reshape(block.shape)
    edges[...] = z_ref[:, plan.mx + plan.rows :, :].astype(F32).reshape(edges.shape)
    fill_taps(plan, block, edges, paired, taps)
    kernel_ref = held["kernel"]
    weights = [
        jnp.concatenate(
            [kernel_ref[2 - a, 2 - b].astype(F32).T for b in range(3)], 1
        ).astype(BF16)
        for a in range(3)
    ]
    convolve(plan, weights, taps, block)
    grad_ref[...] = cot_ref[...].astype(F32) + block[...].reshape(c, bx, by)
    terms = jnp.concatenate(
        [dot_nt(taps[:, a * by : (a + bx) * by], flat[...]) for a in range(3)], 0
    )
    half = terms.shape[0] // 2
    terms = jnp.concatenate([terms[:half], terms[half:]], 1)
    edges[...] = jnp.zeros(edges.shape, F32)
    for t in range(half // s):
        edges[pl.ds(t, s, stride=EDGE), :] = terms[t * s : (t + 1) * s]
    both_ref[:, plan.mx :, :] = edges[...].reshape(s, EDGE, by).astype(BF16)


def end_kernel(plan, held, last_ref, grad_ref, out_ref, kernel_ref, edges):
    c, bx, by, s = plan.channels, plan.bx, plan.by, plan.devices
    edges[...] = last_ref[:, plan.rows :, :].astype(F32).reshape(edges.shape)
    count = 9 * c // (2 * s)
    for t in range(count):
        rows = edges[pl.ds(t, s, stride=EDGE), :]
        for h in range(2):
            start = (h * count + t) * s
            tap, first = start // c, start % c
            a, b = 2 - tap // 3, 2 - tap % 3
            kernel_ref[a, b, first : first + s, :] = rows[:, h * c : (h + 1) * c]
    syn = last_ref[:, : plan.rows, :].astype(F32).reshape(c, bx, by)
    out_ref[...] = (grad_ref[...] + syn).astype(BF16)


def fast_body(plan, field, spectral_weight, kernel_weight, cotangent):
    channels, bx, by, n, cpd = plan.channels, plan.bx, plan.by, plan.devices, plan.cpd
    anywhere = pl.BlockSpec(memory_space=pl.ANY)
    here = pl.BlockSpec(memory_space=pltpu.VMEM)

    def exchange(x):
        return lax.all_to_all(x, BOTH, 0, 0, tiled=True)

    def rows_of(count):
        return jax.ShapeDtypeStruct((n, count, by), BF16)

    def call(
        kernel, outs, *args, us=1.0, scratch=(), mib=56, raw=(), use=(), after=(), spec=None,
        alias=False,
    ):
        several = isinstance(outs, tuple)
        outs = outs if several else (outs,)
        steps = (len(raw), len(args), len(use), len(after))

        def run(*refs):
            groups = []
            for step in steps:
                groups.append(refs[:step])
                refs = refs[step:]
            kernel(plan, dict(zip(use, groups[2])), *groups[0], *groups[1], *refs)

        results = pl.pallas_call(
            run,
            out_shape=outs,
            in_specs=[anywhere] * len(raw)
            + [here] * (len(args) + len(use))
            + [anywhere] * len(after),
            out_specs=(spec or here,) * len(outs),
            scratch_shapes=scratch,
            input_output_aliases={sum(steps) - 1: 0} if alias else {},
            cost_estimate=pl.CostEstimate(
                flops=int(us * 1.0e9), bytes_accessed=1024, transcendentals=0
            ),
            compiler_params=pltpu.CompilerParams(vmem_limit_bytes=mib * 1024 * 1024),
        )(*raw, *args, *(held[name] for name in use), *after)
        return results if several else results[0]

    flat = pltpu.VMEM((n * plan.mx, plan.lanes), F32)
    turned = pltpu.VMEM((plan.mx, channels, 2 * plan.my), F32)
    rows = pltpu.VMEM((plan.mx, 2 * plan.my, channels), F32)
    block = pltpu.VMEM((channels * bx, by), F32)
    edges = pltpu.VMEM((n * EDGE, by), F32)
    paired = pltpu.VMEM((channels, by), F32)
    taps = pltpu.VMEM((3 * channels, (bx + 2) * by), BF16)
    place = pltpu.VMEM(field.shape, BF16)
    kernel_place = pltpu.VMEM(kernel_weight.shape, BF16)
    field_flat = pltpu.VMEM((channels, bx * by), BF16)
    modes_scratch = [
        flat,
        turned,
        rows,
        pltpu.VMEM((plan.mx, plan.my, channels, 2 * channels), BF16),
        pltpu.SemaphoreType.DMA((plan.mx // CHUNK,)),
    ]
    edge_tables = ("pick_rows", "pick_cols", "window")

    field_c = exchange(field.reshape(n, plan.rows, by))
    sources = {name: jnp.asarray(t) for name, t in plan.named().items()}
    packed_shape = (plan.mx, plan.my, channels, 2 * channels)
    half = plan.mx // 2
    chunk_sems = pltpu.SemaphoreType.DMA((half // CHUNK,))
    pack_scratch = [
        pltpu.VMEM((2, half) + packed_shape[1:-1] + (channels,), BF16),
        pltpu.VMEM((half,) + packed_shape[1:], BF16),
    ]
    weights, *held = pl.pallas_call(
        partial(load_kernel, plan, half),
        out_shape=(jax.ShapeDtypeStruct(packed_shape, BF16),)
        + tuple(pltpu.VMEM(t.shape, t.dtype) for t in sources.values()),
        in_specs=[anywhere] * (1 + len(sources)),
        out_specs=(anywhere,) + (here,) * len(sources),
        scratch_shapes=pack_scratch
        + [pltpu.SemaphoreType.DMA((len(sources),)), chunk_sems, chunk_sems],
        cost_estimate=pl.CostEstimate(flops=5_000_000_000, bytes_accessed=1024, transcendentals=0),
        compiler_params=pltpu.CompilerParams(vmem_limit_bytes=58 * 1024 * 1024),
    )(spectral_weight, *sources.values())
    held = dict(zip(sources, held))
    a_part = call(
        first_kernel,
        rows_of(plan.mx + EDGE),
        field_c,
        use=("col", "row") + edge_tables,
        mib=20,
    )
    a_both = exchange(a_part)
    weights = call(
        lambda plan, held, r_ref, after_ref, first_ref, *refs: pack_rows(
            plan, half, half, r_ref, *refs
        ),
        jax.ShapeDtypeStruct(packed_shape, BF16),
        raw=(spectral_weight, a_part, weights),
        scratch=pack_scratch + [chunk_sems, chunk_sems],
        spec=anywhere,
        us=5.0,
        alias=True,
    )
    b_part, a_kept = call(
        mix_kernel,
        (rows_of(plan.mx + 2 * plan.rows), rows_of(plan.mx)),
        a_both,
        raw=(weights, field, cotangent.reshape(n, plan.rows, by), kernel_weight),
        scratch=[place, kernel_place, pltpu.SemaphoreType.DMA((2,))]
        + [block, edges, paired, taps]
        + modes_scratch
        + [pltpu.SemaphoreType.DMA],
        us=6.0,
        mib=54,
    )
    g_part = call(
        middle_kernel,
        rows_of(plan.mx + plan.rows + EDGE),
        exchange(b_part),
        use=("row_s", "col", "row") + edge_tables,
        mib=20,
        scratch=[pltpu.VMEM((plan.nx, cpd * plan.ny), BF16)],
        us=2.6,
    )
    g_both = exchange(g_part)
    layer_out, grad_sum, back_terms, g_kept = call(
        back_kernel,
        (
            jax.ShapeDtypeStruct(field.shape, BF16),
            jax.ShapeDtypeStruct(field.shape, F32),
            rows_of(plan.mx + EDGE),
            rows_of(plan.mx),
        ),
        g_both,
        raw=(weights, field, cotangent, kernel_weight),
        scratch=[place, place, kernel_place, pltpu.SemaphoreType.DMA((3,))]
        + [block, edges, paired, taps, field_flat]
        + modes_scratch,
        us=8.0,
        mib=54,
    )
    back_both = exchange(back_terms)

    def outer_part(first_j, count, after, alias):
        return call(
            lambda plan, *refs: outer_kernel(plan, first_j, count, *refs),
            jax.ShapeDtypeStruct(spectral_weight.shape, BF16),
            a_kept,
            g_kept,
            scratch=[
                flat,
                flat,
                turned,
                turned,
                pltpu.VMEM((2, count, plan.my, channels, channels), BF16),
                pltpu.SemaphoreType.DMA((count // CHUNK,)),
            ],
            spec=anywhere,
            us=6.4,
            after=after,
            alias=alias,
        )

    spectral_half = outer_part(0, half, (back_terms,), False)
    last_part = call(
        last_kernel,
        rows_of(plan.rows + EDGE),
        back_both,
        use=("row_s", "col"),
        us=1.3,
        mib=44,
        after=(spectral_half,),
    )
    last_both = exchange(last_part)
    spectral_grad = outer_part(half, half, (last_part, spectral_half), True)
    field_grad, kernel_grad = call(
        end_kernel,
        (
            jax.ShapeDtypeStruct(field.shape, BF16),
            jax.ShapeDtypeStruct((3, 3, channels, channels), F32),
        ),
        last_both,
        grad_sum,
        scratch=[edges],
        mib=20,
    )
    return (layer_out, field_grad, spectral_grad, kernel_grad)


def body(field, spectral_weight, kernel_weight, cotangent):
    plan = Plan(*field.shape, lax.axis_size("gx"), lax.axis_size("gy"))
    if plan.fits:
        return fast_body(plan, field, spectral_weight, kernel_weight, cotangent)
    return general_body(field, spectral_weight, kernel_weight, cotangent)


def solution(mesh):
    in_specs = (P(None, "gx", "gy"), P(None, "gx", "gy", None, None), P(), P(None, "gx", "gy"))
    out_specs = (P(None, "gx", "gy"), P(None, "gx", "gy"), P(None, "gx", "gy", None, None), P())
    return jax.shard_map(body, mesh=mesh, in_specs=in_specs, out_specs=out_specs, check_vma=False)
```

```python
from functools import partial
import math

import jax
import jax.numpy as jnp
import ml_dtypes
import numpy as np
from jax import lax
from jax.experimental import pallas as pl
from jax.experimental.pallas import tpu as pltpu
from jax.sharding import PartitionSpec as P

KX = 128
KY = 128


def extended(array, sides, width):
    for axis, dim in sides:
        count, length = (lax.axis_size(axis), array.shape[dim])
        up = [(i, (i + 1) % count) for i in range(count)]
        down = [(j, i) for i, j in up]
        last = lax.slice_in_dim(array, length - width, length, axis=dim)
        initial = lax.slice_in_dim(array, 0, width, axis=dim)
        before = lax.ppermute(last, axis, up)
        after = lax.ppermute(initial, axis, down)
        array = jnp.concatenate([before, array, after], axis=dim)
    return array


def phases(waves, points, length):
    wrapped = jnp.mod(waves[:, None] * points[None, :], length).astype(jnp.float32)
    return wrapped * (2.0 * math.pi / length)


def widen(field):
    return extended(field, (("gx", 1), ("gy", 2)), 1)


def general_body(field, spectral_weight, kernel_weight, cotangent):
    highest = lax.Precision.HIGHEST
    channels, block_rows, block_cols = field.shape
    rows_total = block_rows * lax.axis_size("gx")
    cols_total = block_cols * lax.axis_size("gy")
    scale = 1.0 / math.sqrt(rows_total * cols_total)
    row_coord = lax.axis_index("gx") * block_rows + jnp.arange(block_rows, dtype=jnp.int32)
    col_coord = lax.axis_index("gy") * block_cols + jnp.arange(block_cols, dtype=jnp.int32)
    modes_x = KX // lax.axis_size("gx")
    modes_y = KY // lax.axis_size("gy")

    def analyse(source):
        waves = jnp.arange(lax.axis_size("gy") * modes_y, dtype=jnp.int32)
        angles = phases(waves, col_coord, cols_total)
        table = jnp.concatenate([jnp.cos(angles), -jnp.sin(angles)], 0).astype(jnp.bfloat16)
        product = jnp.dot(
            source.reshape(channels * block_rows, block_cols),
            table.T,
            preferred_element_type=jnp.float32,
        )
        product = product.reshape(channels, block_rows, 2, lax.axis_size("gy") * modes_y).transpose(
            3, 1, 2, 0
        )
        col_modes = lax.psum_scatter(
            product.reshape(lax.axis_size("gy") * modes_y, block_rows, 2 * channels),
            "gy",
            scatter_dimension=0,
            tiled=True,
        )
        split_modes = col_modes.reshape(modes_y, block_rows, 2, channels)
        real_in = split_modes[:, :, 0]
        imag_in = split_modes[:, :, 1]
        waves = jnp.arange(lax.axis_size("gx") * modes_x, dtype=jnp.int32) - KX // 2
        angles = phases(waves, row_coord, rows_total)
        cosines = jnp.cos(angles)
        sines = jnp.sin(angles)
        contract = partial(jnp.einsum, "jx,lxc->jlc", precision=highest)
        real_out = contract(cosines, real_in) + contract(sines, imag_in)
        imag_out = contract(cosines, imag_in) - contract(sines, real_in)
        return lax.psum_scatter(
            jnp.stack([real_out, imag_out], 2).reshape(
                lax.axis_size("gx") * modes_x, modes_y, 2 * channels
            )
            * scale,
            "gx",
            scatter_dimension=0,
            tiled=True,
        ).reshape(modes_x, modes_y, 2, channels)

    def synthesise(modes):
        start_rows = jnp.zeros((modes_y, block_rows, 2 * channels), jnp.float32)
        shard_rows = lax.all_gather(
            modes.reshape(modes_x, modes_y, 2 * channels), "gx", axis=0, tiled=True
        )
        amount = shard_rows.shape[0]
        waves = jnp.arange(amount, dtype=jnp.int32) - KX // 2
        angles = phases(waves, row_coord, rows_total)
        cosines = jnp.cos(angles).astype(jnp.bfloat16)
        sines = jnp.sin(angles).astype(jnp.bfloat16)
        split_rows = shard_rows.reshape(amount, modes_y, 2, channels)
        real_in = split_rows[:, :, 0]
        imag_in = split_rows[:, :, 1]
        contract = partial(jnp.einsum, "jx,jlc->lxc", preferred_element_type=jnp.float32)
        real_out = contract(cosines, real_in) - contract(sines, imag_in)
        imag_out = contract(sines, real_in) + contract(cosines, imag_in)
        row_sum = start_rows + jnp.stack([real_out, imag_out], 2).reshape(
            modes_y, block_rows, 2 * channels
        )
        row_sum = row_sum.astype(jnp.bfloat16)
        shard_rows = lax.all_gather(row_sum, "gy", axis=0, tiled=True)
        amount = shard_rows.shape[0]
        waves = jnp.arange(amount, dtype=jnp.int32)
        angles = phases(waves, col_coord, cols_total)
        table = jnp.stack([jnp.cos(angles), -jnp.sin(angles)], 1).astype(jnp.bfloat16)
        split_rows = shard_rows.reshape(amount, block_rows, 2, channels)
        return (
            jnp.einsum("lxpc,lpy->cxy", split_rows, table, preferred_element_type=jnp.float32)
            * scale
        )

    padded_field = widen(field)
    hidden = jnp.zeros((channels, block_rows, block_cols), jnp.float32)
    for row_tap in range(3):
        for col_tap in range(3):
            window = padded_field[:, row_tap : row_tap + block_rows, col_tap : col_tap + block_cols]
            hidden = hidden + jnp.einsum(
                "oi,ixy->oxy",
                kernel_weight[row_tap, col_tap],
                window,
                preferred_element_type=jnp.float32,
            )
    amodes = analyse(field)
    areal = amodes[:, :, 0]
    aimag = amodes[:, :, 1]
    wreal = spectral_weight[0].astype(jnp.float32)
    wimag = spectral_weight[1].astype(jnp.float32)
    mixing = partial(jnp.einsum, "jli,jlio->jlo", precision=highest)
    breal = mixing(areal, wreal) - mixing(aimag, wimag)
    bimag = mixing(areal, wimag) + mixing(aimag, wreal)
    wave_index = lax.axis_index("gy") * modes_y + jnp.arange(modes_y, dtype=jnp.int32)
    weights = jnp.where(wave_index == 0, 1.0, 2.0).astype(jnp.float32)[None, :, None, None]
    bmodes = (jnp.stack([breal, bimag], 2) * weights).astype(jnp.bfloat16)
    hidden = hidden + synthesise(bmodes)
    activated, pullback = jax.vjp(jax.nn.gelu, hidden)
    layer_out = (field.astype(jnp.float32) + activated).astype(jnp.bfloat16)
    grads = pullback(cotangent.astype(jnp.float32))[0].astype(jnp.bfloat16)
    gmodes = analyse(grads) * weights
    greal = gmodes[:, :, 0]
    gimag = gmodes[:, :, 1]
    outer = partial(jnp.einsum, "jli,jlo->jlio", precision=highest)
    spectral_grad = jnp.stack(
        [outer(areal, greal) + outer(aimag, gimag), outer(areal, gimag) - outer(aimag, greal)], 0
    ).astype(jnp.bfloat16)
    back = partial(jnp.einsum, "jlio,jlo->jli", precision=highest)
    back_real = back(wreal, greal) + back(wimag, gimag)
    back_imag = back(wreal, gimag) - back(wimag, greal)
    back_modes = jnp.stack([back_real, back_imag], 2).astype(jnp.bfloat16)
    padded_grads = widen(grads)
    adjoint = jnp.zeros((channels, block_rows, block_cols), jnp.float32)
    tap_rows = []
    for row_tap in range(3):
        tap_cols = []
        for col_tap in range(3):
            window = padded_grads[
                :, 2 - row_tap : 2 - row_tap + block_rows, 2 - col_tap : 2 - col_tap + block_cols
            ]
            adjoint = adjoint + jnp.einsum(
                "oi,oxy->ixy",
                kernel_weight[row_tap, col_tap],
                window,
                preferred_element_type=jnp.float32,
            )
            source_window = padded_field[
                :, row_tap : row_tap + block_rows, col_tap : col_tap + block_cols
            ]
            tap_cols.append(
                jnp.einsum("oxy,ixy->oi", grads, source_window, preferred_element_type=jnp.float32)
            )
        tap_rows.append(jnp.stack(tap_cols, 0))
    kernel_grad = lax.psum(jnp.stack(tap_rows, 0), ("gx", "gy"))
    field_grad = (cotangent.astype(jnp.float32) + adjoint + synthesise(back_modes)).astype(
        jnp.bfloat16
    )
    return (layer_out, field_grad, spectral_grad, kernel_grad)


BF16 = jnp.bfloat16
F32 = jnp.float32
BOTH = ("gx", "gy")
EDGE = 16
GROUP = 8
CHUNK = 2
MIXED = 8


class Plan:
    def __init__(self, channels, block_rows, block_cols, gx, gy):
        self.gx, self.gy, self.devices = gx, gy, gx * gy
        self.channels, self.bx, self.by = channels, block_rows, block_cols
        self.nx, self.ny = block_rows * gx, block_cols * gy
        self.mx, self.my = KX // gx, KY // gy
        self.cpd = channels // self.devices if channels % self.devices == 0 else 0
        self.lanes = self.cpd * 2 * self.my
        self.rows = self.cpd * self.bx
        self.fits = (
            self.cpd == 2
            and channels == 64
            and self.lanes == 128
            and self.by == 128
            and self.bx == 16
            and KX % gx == 0
            and KY % gy == 0
            and self.mx == 16
            and self.my % GROUP == 0
            and gy % 2 == 0
            and KX == 128
            and self.nx == 128
        )
        self.scale = 1.0 / math.sqrt(self.nx * self.ny)

    def tables(self):
        two_pi = np.float32(2.0 * math.pi)
        waves, points = np.arange(KY), np.arange(self.ny)
        angles = np.float32((waves[:, None] * points[None, :]) % self.ny) * (two_pi / self.ny)
        cos, sin = np.cos(angles).T, np.sin(angles).T
        split = (self.ny, self.gy, self.my)
        cos, sin = cos.reshape(split), sin.reshape(split)
        top, bottom = np.stack([cos, -sin], 2), np.stack([-sin, -cos], 2)
        col = np.stack([top, bottom], 1).reshape(self.ny, -1).astype(ml_dtypes.bfloat16)
        rows = np.arange(KX) - KX // 2
        points = np.arange(self.nx)
        angles = np.float32((rows[:, None] * points[None, :]) % self.nx) * (two_pi / self.nx)
        row = np.concatenate([np.cos(angles), np.sin(angles)], 1).astype(np.float32)
        high = row.astype(ml_dtypes.bfloat16)
        low = (row - high.astype(np.float32)).astype(ml_dtypes.bfloat16)
        row_analysis = np.concatenate([high, low], 1)
        row_synthesis = np.concatenate([np.cos(angles).T, np.sin(angles).T], 0)
        row_synthesis = row_synthesis.astype(ml_dtypes.bfloat16)
        return col, row_analysis, row_synthesis

    def named(self):
        names = ("col", "row", "row_s", "pick_rows", "pick_cols", "window")
        return dict(zip(names, self.tables() + self.pickers()))

    def pickers(self):
        pick_rows = np.zeros((self.gx, EDGE, self.cpd, self.nx), np.float32)
        pick_cols = np.zeros((self.gy, EDGE, self.cpd, self.ny), np.float32)
        window = np.zeros((self.nx, self.gx, self.by), np.float32)
        for c in range(self.cpd):
            for g in range(self.gx):
                pick_rows[g, 2 * c, c, (g * self.bx - 1) % self.nx] = 1
                pick_rows[g, 2 * c + 1, c, ((g + 1) * self.bx) % self.nx] = 1
            for g in range(self.gy):
                pick_cols[g, 2 * self.cpd + 2 * c, c, (g * self.by - 1) % self.ny] = 1
                pick_cols[g, 2 * self.cpd + 2 * c + 1, c, ((g + 1) * self.by) % self.ny] = 1
        for g in range(self.gx):
            for t in range(self.bx + 2):
                window[(g * self.bx - 1 + t) % self.nx, g, t] = 1
        kind = ml_dtypes.bfloat16
        return (
            pick_rows.reshape(self.gx * EDGE, -1).astype(kind),
            pick_cols.reshape(self.gy * EDGE, -1).astype(kind),
            window.reshape(self.nx, -1).astype(kind),
        )


def dot(a, b):
    return jnp.dot(a, b, preferred_element_type=F32)


def dot_nt(a, b):
    return lax.dot_general(a, b, (((1,), (1,)), ((), ())), preferred_element_type=F32)


def interleave(plan, parts):
    half = plan.lanes // 2
    lane = lax.broadcasted_iota(jnp.int32, (1, plan.lanes), 1)
    tiles = []
    for k in range(plan.gy // 2):
        first, second = (p[:, k * plan.lanes : (k + 1) * plan.lanes] for p in parts)
        tiles.append(jnp.where(lane < half, first, pltpu.roll(second, half, 1)))
        tiles.append(jnp.where(lane < half, pltpu.roll(first, half, 1), second))
    return jnp.concatenate(tiles, 1)


def separate(plan, values):
    half = plan.lanes // 2
    lane = lax.broadcasted_iota(jnp.int32, (1, plan.lanes), 1)
    parts = ([], [])
    for k in range(plan.gy // 2):
        even = values[:, 2 * k * plan.lanes : (2 * k + 1) * plan.lanes]
        odd = values[:, (2 * k + 1) * plan.lanes : (2 * k + 2) * plan.lanes]
        parts[0].append(jnp.where(lane < half, even, pltpu.roll(odd, half, 1)))
        parts[1].append(jnp.where(lane < half, pltpu.roll(even, half, 1), odd))
    return [jnp.concatenate(p, 1) for p in parts]


def analyse_plane(plan, held, planes, weight, out_ref):
    col = held["col"]
    half = col.shape[1] // 2
    along_y = [
        dot(planes[:, c * plan.ny : (c + 1) * plan.ny], col[...]) for c in range(plan.cpd)
    ]
    stacked = jnp.concatenate(
        [
            interleave(plan, [p[:, :half] for p in along_y]),
            interleave(plan, [p[:, half:] for p in along_y]),
        ],
        0,
    ).astype(BF16)
    modes = dot(held["row"][...], jnp.concatenate([stacked, stacked], 0)) * weight
    modes = modes.astype(BF16)
    for i in range(plan.gx):
        for k in range(plan.gy):
            out_ref[i * plan.gy + k, : plan.mx] = modes[
                i * plan.mx : (i + 1) * plan.mx, k * plan.lanes : (k + 1) * plan.lanes
            ]


def put_edges(plan, held, planes, out_ref, start):
    stacked = jnp.concatenate(
        [planes[:, c * plan.ny : (c + 1) * plan.ny] for c in range(plan.cpd)], 0
    )
    edge_rows = dot(held["pick_rows"][...], stacked)
    picked = dot_nt(held["pick_cols"][...], planes).astype(BF16)
    edge_cols = dot(picked, held["window"][...])
    for i in range(plan.gx):
        for k in range(plan.gy):
            tile = (
                edge_rows[i * EDGE : (i + 1) * EDGE, k * plan.by : (k + 1) * plan.by]
                + edge_cols[k * EDGE : (k + 1) * EDGE, i * plan.by : (i + 1) * plan.by]
            )
            out_ref[i * plan.gy + k, start : start + EDGE] = tile.astype(BF16)


def synthesise_plane(plan, held, modes_ref, weight):
    columns = []
    for k in range(plan.gy):
        columns.append(
            jnp.concatenate([modes_ref[i * plan.gy + k, : plan.mx] for i in range(plan.gx)], 0)
        )
    sums = dot(held["row_s"][...], jnp.concatenate(columns, 1))
    if weight is not None:
        sums = sums * weight
    top, bottom = separate(plan, sums[: plan.nx]), separate(plan, sums[plan.nx :])
    planes = []
    for c in range(plan.cpd):
        left = jnp.concatenate([top[c], bottom[c]], 1).astype(BF16)
        planes.append(dot_nt(left, held["col"][...]))
    return jnp.concatenate(planes, 1)


def read_plane(plan, ref, c, k, first=0):
    rows = slice(first + c * plan.bx, first + (c + 1) * plan.bx)
    return jnp.concatenate([ref[i * plan.gy + k, rows] for i in range(plan.gx)], 0)


def write_plane(plan, ref, c, k, values, first=0):
    rows = slice(first + c * plan.bx, first + (c + 1) * plan.bx)
    for i in range(plan.gx):
        ref[i * plan.gy + k, rows] = values[i * plan.bx : (i + 1) * plan.bx]


def first_kernel(plan, held, field_ref, out_ref):
    planes = jnp.concatenate(
        [read_plane(plan, field_ref, c, k) for c in range(plan.cpd) for k in range(plan.gy)], 1
    )
    analyse_plane(plan, held, planes, plan.scale, out_ref)
    put_edges(plan, held, planes, out_ref, plan.mx)


def gelu_parts(z):
    factor = math.sqrt(2.0 / math.pi)
    tanh = jnp.tanh(factor * (z + 0.044715 * (z * z * z)))
    cdf = 0.5 * (1.0 + tanh)
    slope = cdf + 0.5 * z * (1.0 - tanh * tanh) * (factor * (1.0 + (3.0 * 0.044715) * (z * z)))
    return z * cdf, slope


def middle_kernel(plan, held, modes_ref, out_ref, grads):
    lane = lax.broadcasted_iota(jnp.int32, (1, plan.gy * plan.lanes), 1)
    zero = jnp.logical_and(lane < plan.lanes, lax.rem(lane, plan.my) == 0)
    doubled = jnp.where(zero, 1.0, 2.0)
    syn = synthesise_plane(plan, held, modes_ref, doubled) * plan.scale
    for c in range(plan.cpd):
        for k in range(plan.gy):
            start = c * plan.ny + k * plan.by
            z = syn[:, start : start + plan.by] + read_plane(plan, modes_ref, c, k, plan.mx).astype(F32)
            z = z.astype(BF16)
            write_plane(plan, out_ref, c, k, z, plan.mx)
            slope = gelu_parts(z.astype(F32))[1]
            cot = read_plane(plan, modes_ref, plan.cpd + c, k, plan.mx).astype(F32)
            grads[:, start : start + plan.by] = (cot * slope).astype(BF16)
    planes = grads[...]
    analyse_plane(plan, held, planes, doubled * plan.scale, out_ref)
    put_edges(plan, held, planes, out_ref, plan.mx + plan.rows)


def last_kernel(plan, held, both_ref, out_ref):
    syn = synthesise_plane(plan, held, both_ref, None) * plan.scale
    syn = syn.astype(BF16)
    for c in range(plan.cpd):
        for k in range(plan.gy):
            start = c * plan.ny + k * plan.by
            write_plane(plan, out_ref, c, k, syn[:, start : start + plan.by])
    terms = both_ref[0, plan.mx :].astype(F32)
    for s in range(1, plan.devices):
        terms = terms + both_ref[s, plan.mx :].astype(F32)
    terms = terms.astype(BF16)
    for s in range(plan.devices):
        out_ref[s, plan.rows :] = terms


def gather_modes(plan, x_ref, flat, turned, j):
    s, half = plan.devices, plan.lanes // 2
    values = flat[pl.ds(j, s, stride=plan.mx), :]
    for c in range(plan.cpd):
        turned[j, pl.ds(c, s, stride=plan.cpd), :] = values[:, c * half : (c + 1) * half]


def spread(plan, x_ref, flat):
    flat[...] = x_ref[:, : plan.mx, :].astype(F32).reshape(plan.devices * plan.mx, plan.lanes)


def modes_to_rows(plan, x_ref, flat, turned, rows):
    spread(plan, x_ref, flat)
    for j in range(plan.mx):
        gather_modes(plan, x_ref, flat, turned, j)
        rows[j] = turned[j].T


def rows_to_modes(plan, values, turned, flat, j):
    s = plan.devices
    turned[j] = values.T
    parts = [turned[j, pl.ds(c, s, stride=plan.cpd), :] for c in range(plan.cpd)]
    flat[pl.ds(j, s, stride=plan.mx), :] = jnp.concatenate(parts, 1)


def group_mask(rows, groups, width):
    row = lax.broadcasted_iota(jnp.int32, (rows, groups * width), 0)
    lane = lax.broadcasted_iota(jnp.int32, (rows, groups * width), 1)
    return lax.rem(row, groups) == lax.div(lane, width)


def pack_rows(plan, first_j, count, r_ref, packed_ref, arrived, packed, in_sems, out_sems, others=()):
    chunks = count // CHUNK

    def part(t, start=0):
        return pl.ds(start + t * CHUNK, CHUNK)

    loads = [
        pltpu.make_async_copy(r_ref.at[:, part(t, first_j)], arrived.at[:, part(t)], in_sems.at[t])
        for t in range(chunks)
    ]
    stores = [
        pltpu.make_async_copy(packed.at[part(t)], packed_ref.at[part(t, first_j)], out_sems.at[t])
        for t in range(chunks)
    ]
    for copy in loads + list(others):
        copy.start()
    for t in range(chunks):
        loads[t].wait()
        for j in range(t * CHUNK, (t + 1) * CHUNK):
            packed[j] = jnp.concatenate([arrived[0, j], arrived[1, j]], -1)
        stores[t].start()
    for copy in list(others) + stores:
        copy.wait()


def load_kernel(plan, half, *refs):
    count = (len(refs) - 7) // 2
    r_ref, sources = refs[0], refs[1 : 1 + count]
    packed_ref, places = refs[1 + count], refs[2 + count : 2 + 2 * count]
    arrived, packed, sems, in_sems, out_sems = refs[2 + 2 * count :]
    copies = [
        pltpu.make_async_copy(source, place, sems.at[i])
        for i, (source, place) in enumerate(zip(sources, places))
    ]
    pack_rows(plan, 0, half, r_ref, packed_ref, arrived, packed, in_sems, out_sems, copies)


def each_mode_row(plan, product, first, mixed, r_ref, x_ref, y_ref, flat, turned, rows, held, sems):
    width = plan.channels
    copies = [
        pltpu.make_async_copy(
            r_ref.at[pl.ds(t * mixed, mixed)], held.at[pl.ds(t * mixed, mixed)], sems.at[t]
        )
        for t in range(plan.mx // mixed)
    ]
    for copy in copies:
        copy.start()
    modes_to_rows(plan, x_ref, flat, turned, rows)
    first()
    mask = group_mask(2 * GROUP, GROUP, width)

    def step(j, carry):
        real_out, imag_out = [], []
        for g in range(plan.my // GROUP):
            start = g * GROUP
            real = rows[j, start : start + GROUP, :]
            imag = rows[j, plan.my + start : plan.my + start + GROUP, :]
            weights = held[j, start : start + GROUP].reshape(GROUP * width, 2 * width)
            real, imag = product(mask, real, imag, weights)
            real_out.append(real)
            imag_out.append(imag)
        rows_to_modes(plan, jnp.concatenate(real_out + imag_out, 0), turned, flat, j)
        return carry

    for t, copy in enumerate(copies):
        copy.wait()
        lax.fori_loop(t * mixed, (t + 1) * mixed, step, 0, unroll=16 if mixed == 16 else 8)
    values = flat[...].reshape(plan.devices, plan.mx, plan.lanes)
    y_ref[:, : plan.mx] = values.astype(BF16)


class Arrival:
    def __init__(self, source, place, sem):
        self.copy, self.place, self.there = pltpu.make_async_copy(source, place, sem), place, False
        self.copy.start()

    def __getitem__(self, index):
        if not self.there:
            self.copy.wait()
            self.there = True
        return self.place[index]


def bring(sources, refs):
    count = len(sources)
    arrivals = {
        name: Arrival(source, refs[i], refs[count].at[i])
        for i, (name, source) in enumerate(sources)
    }
    return arrivals, refs[count + 1 :]


def mix_kernel(plan, held, r_ref, field_ref, cot_ref, kernel_ref, x_ref, y_ref, kept_ref, *refs):
    kept_ref[...] = x_ref[:, : plan.mx]
    width = plan.channels
    held, refs = bring((("field", field_ref), ("kernel", kernel_ref)), refs)
    cot = pltpu.make_async_copy(cot_ref, y_ref.at[:, pl.ds(plan.mx + plan.rows, plan.rows)], refs[-1])
    cot.start()
    refs = refs[:-1]

    def product(mask, real, imag, weights):
        left = jnp.concatenate([jnp.concatenate([real, imag], 0)] * GROUP, 1)
        mixed = dot(jnp.where(mask, left, 0.0).astype(BF16), weights)
        return (
            mixed[:GROUP, :width] - mixed[GROUP:, width:],
            mixed[:GROUP, width:] + mixed[GROUP:, :width],
        )

    conv = partial(conv_part, plan, held, x_ref, y_ref, *refs[:4])
    each_mode_row(plan, product, conv, MIXED, r_ref, x_ref, y_ref, *refs[4:])
    cot.wait()


def back_kernel(
    plan, held, r_ref, field_ref, cot_ref, kernel_ref, g_ref, layer_ref, grad_ref, both_ref,
    kept_ref, *refs
):
    kept_ref[...] = g_ref[:, : plan.mx]
    width = plan.channels
    sources = (("field", field_ref), ("cotangent", cot_ref), ("kernel", kernel_ref))
    held, refs = bring(sources, refs)

    def product(mask, real, imag, weights):
        left = jnp.concatenate(
            [jnp.concatenate([real, imag], 1), jnp.concatenate([imag, -real], 1)], 0
        )
        mixed = jnp.where(mask, dot_nt(left.astype(BF16), weights), 0.0)
        total = mixed[:, : 2 * width]
        for i in range(1, GROUP // 2):
            total = total + mixed[:, 2 * i * width : 2 * (i + 1) * width]
        total = total[:, :width] + total[:, width:]
        return total[:GROUP], total[GROUP:]

    space = partial(space_part, plan, held, g_ref, layer_ref, grad_ref, both_ref, *refs[:5])
    each_mode_row(plan, product, space, plan.mx, r_ref, g_ref, both_ref, *refs[5:])


def outer_kernel(
    plan, first_j, count, held, x_ref, g_ref, *refs
):
    out_ref, x_flat, g_flat, a_turned, g_turned, slots, sems = refs
    my, width = plan.my, plan.channels
    spread(plan, x_ref, x_flat)
    spread(plan, g_ref, g_flat)
    for j in range(first_j, first_j + count):
        gather_modes(plan, x_ref, x_flat, a_turned, j)
        gather_modes(plan, g_ref, g_flat, g_turned, j)
    lane = lax.rem(lax.broadcasted_iota(jnp.int32, (width, 2 * my), 1), my)
    copies = []
    for j in range(first_j, first_j + count):
        left = a_turned[j]
        g_rows = g_turned[j].T
        g_real, g_imag = g_rows[:my], g_rows[my:]
        right = jnp.concatenate(
            [jnp.concatenate([g_real, g_imag], 1), jnp.concatenate([g_imag, -g_real], 1)], 0
        ).astype(BF16)
        for g in range(my // GROUP):
            picked = jnp.concatenate(
                [jnp.where(lane == g * GROUP + l, left, 0.0) for l in range(GROUP)], 0
            ).astype(BF16)
            value = dot(picked, right).astype(BF16)
            for part in range(2):
                slots[part, j - first_j, g * GROUP : (g + 1) * GROUP] = value[
                    :, part * width : (part + 1) * width
                ].reshape(GROUP, width, width)
        if (j + 1) % CHUNK == 0:
            t = (j + 1 - first_j) // CHUNK - 1
            copies.append(
                pltpu.make_async_copy(
                    slots.at[:, pl.ds(t * CHUNK, CHUNK)],
                    out_ref.at[:, pl.ds(first_j + t * CHUNK, CHUNK)],
                    sems.at[t],
                )
            )
            copies[-1].start()
    for copy in copies:
        copy.wait()


def fill_taps(plan, block, edges, paired, taps):
    c, bx, by, s = plan.channels, plan.bx, plan.by, plan.devices

    def edge(first):
        for p in range(plan.cpd):
            paired[pl.ds(p, s, stride=plan.cpd), :] = edges[
                pl.ds(first + 2 * p, s, stride=EDGE), :
            ]
        return paired[...]

    top, bottom = edge(0), edge(1)
    left, right = edge(2 * plan.cpd), edge(2 * plan.cpd + 1)
    lane = lax.broadcasted_iota(jnp.int32, (c, by), 1)
    for x in range(bx + 2):
        if x == 0:
            row = top
        elif x == bx + 1:
            row = bottom
        else:
            row = block[pl.ds(x - 1, c, stride=bx), :]
        lanes = slice(x * by, (x + 1) * by)
        taps[:c, lanes] = jnp.where(
            lane == 0, left[:, x : x + 1], pltpu.roll(row, 1, 1)
        ).astype(BF16)
        taps[c : 2 * c, lanes] = row.astype(BF16)
        taps[2 * c :, lanes] = jnp.where(
            lane == by - 1, right[:, x : x + 1], pltpu.roll(row, by - 1, 1)
        ).astype(BF16)


def convolve(plan, weights, taps, out):
    bx, by = plan.bx, plan.by
    total = dot(weights[0], taps[:, : bx * by])
    for a in range(1, 3):
        total = total + dot(weights[a], taps[:, a * by : (a + bx) * by])
    for x in range(bx):
        out[pl.ds(x, plan.channels, stride=bx), :] = total[:, x * by : (x + 1) * by]


def conv_part(plan, held, both_ref, out_ref, block, edges, paired, taps):
    edges[...] = both_ref[:, plan.mx :, :].astype(F32).reshape(edges.shape)
    block[...] = held["field"][...].astype(F32).reshape(block.shape)
    fill_taps(plan, block, edges, paired, taps)
    kernel_ref = held["kernel"]
    weights = [jnp.concatenate([kernel_ref[a, b] for b in range(3)], 1) for a in range(3)]
    convolve(plan, weights, taps, block)
    shape = (plan.devices, plan.rows, plan.by)
    out_ref[:, plan.mx : plan.mx + plan.rows] = block[...].reshape(shape).astype(BF16)


def space_part(
    plan, held, z_ref, layer_ref, grad_ref, both_ref, block, edges, paired, taps, flat
):
    c, bx, by, s = plan.channels, plan.bx, plan.by, plan.devices
    z = z_ref[:, plan.mx : plan.mx + plan.rows, :].astype(F32).reshape(c, bx, by)
    activated, slope = gelu_parts(z)
    field = held["field"][...].astype(F32)
    layer_ref[...] = (field + activated).astype(BF16)
    block[...] = field.reshape(block.shape)
    for x in range(bx):
        flat[:, x * by : (x + 1) * by] = block[pl.ds(x, c, stride=bx), :].astype(BF16)
    cot_ref = held["cotangent"]
    grads = (cot_ref[...].astype(F32) * slope).astype(BF16).astype(F32)
    block[...] = grads.reshape(block.shape)
    edges[...] = z_ref[:, plan.mx + plan.rows :, :].astype(F32).reshape(edges.shape)
    fill_taps(plan, block, edges, paired, taps)
    kernel_ref = held["kernel"]
    weights = [
        jnp.concatenate(
            [kernel_ref[2 - a, 2 - b].astype(F32).T for b in range(3)], 1
        ).astype(BF16)
        for a in range(3)
    ]
    convolve(plan, weights, taps, block)
    grad_ref[...] = cot_ref[...].astype(F32) + block[...].reshape(c, bx, by)
    terms = jnp.concatenate(
        [dot_nt(taps[:, a * by : (a + bx) * by], flat[...]) for a in range(3)], 0
    )
    half = terms.shape[0] // 2
    terms = jnp.concatenate([terms[:half], terms[half:]], 1)
    edges[...] = jnp.zeros(edges.shape, F32)
    for t in range(half // s):
        edges[pl.ds(t, s, stride=EDGE), :] = terms[t * s : (t + 1) * s]
    both_ref[:, plan.mx :, :] = edges[...].reshape(s, EDGE, by).astype(BF16)


def end_kernel(plan, held, last_ref, grad_ref, out_ref, kernel_ref, edges):
    c, bx, by, s = plan.channels, plan.bx, plan.by, plan.devices
    edges[...] = last_ref[:, plan.rows :, :].astype(F32).reshape(edges.shape)
    count = 9 * c // (2 * s)
    for t in range(count):
        rows = edges[pl.ds(t, s, stride=EDGE), :]
        for h in range(2):
            start = (h * count + t) * s
            tap, first = start // c, start % c
            a, b = 2 - tap // 3, 2 - tap % 3
            kernel_ref[a, b, first : first + s, :] = rows[:, h * c : (h + 1) * c]
    syn = last_ref[:, : plan.rows, :].astype(F32).reshape(c, bx, by)
    out_ref[...] = (grad_ref[...] + syn).astype(BF16)


def fast_body(plan, field, spectral_weight, kernel_weight, cotangent):
    channels, bx, by, n, cpd = plan.channels, plan.bx, plan.by, plan.devices, plan.cpd
    anywhere = pl.BlockSpec(memory_space=pl.ANY)
    here = pl.BlockSpec(memory_space=pltpu.VMEM)

    def exchange(x):
        return lax.all_to_all(x, BOTH, 0, 0, tiled=True)

    def rows_of(count):
        return jax.ShapeDtypeStruct((n, count, by), BF16)

    def call(
        kernel, outs, *args, us=1.0, scratch=(), mib=56, raw=(), use=(), after=(), spec=None,
        alias=False,
    ):
        several = isinstance(outs, tuple)
        outs = outs if several else (outs,)
        steps = (len(raw), len(args), len(use), len(after))

        def run(*refs):
            groups = []
            for step in steps:
                groups.append(refs[:step])
                refs = refs[step:]
            kernel(plan, dict(zip(use, groups[2])), *groups[0], *groups[1], *refs)

        results = pl.pallas_call(
            run,
            out_shape=outs,
            in_specs=[anywhere] * len(raw)
            + [here] * (len(args) + len(use))
            + [anywhere] * len(after),
            out_specs=(spec or here,) * len(outs),
            scratch_shapes=scratch,
            input_output_aliases={sum(steps) - 1: 0} if alias else {},
            cost_estimate=pl.CostEstimate(
                flops=int(us * 1.0e9), bytes_accessed=1024, transcendentals=0
            ),
            compiler_params=pltpu.CompilerParams(vmem_limit_bytes=mib * 1024 * 1024),
        )(*raw, *args, *(held[name] for name in use), *after)
        return results if several else results[0]

    flat = pltpu.VMEM((n * plan.mx, plan.lanes), F32)
    turned = pltpu.VMEM((plan.mx, channels, 2 * plan.my), F32)
    rows = pltpu.VMEM((plan.mx, 2 * plan.my, channels), F32)
    block = pltpu.VMEM((channels * bx, by), F32)
    edges = pltpu.VMEM((n * EDGE, by), F32)
    paired = pltpu.VMEM((channels, by), F32)
    taps = pltpu.VMEM((3 * channels, (bx + 2) * by), BF16)
    place = pltpu.VMEM(field.shape, BF16)
    kernel_place = pltpu.VMEM(kernel_weight.shape, BF16)
    field_flat = pltpu.VMEM((channels, bx * by), BF16)
    modes_scratch = [
        flat,
        turned,
        rows,
        pltpu.VMEM((plan.mx, plan.my, channels, 2 * channels), BF16),
        pltpu.SemaphoreType.DMA((plan.mx // CHUNK,)),
    ]
    edge_tables = ("pick_rows", "pick_cols", "window")

    field_c = exchange(field.reshape(n, plan.rows, by))
    sources = {name: jnp.asarray(t) for name, t in plan.named().items()}
    packed_shape = (plan.mx, plan.my, channels, 2 * channels)
    half = plan.mx // 2
    early, late = half - CHUNK, half + CHUNK
    chunk_sems = pltpu.SemaphoreType.DMA((late // CHUNK,))
    pack_scratch = [
        pltpu.VMEM((2, late) + packed_shape[1:-1] + (channels,), BF16),
        pltpu.VMEM((late,) + packed_shape[1:], BF16),
    ]
    weights, *held = pl.pallas_call(
        partial(load_kernel, plan, early),
        out_shape=(jax.ShapeDtypeStruct(packed_shape, BF16),)
        + tuple(pltpu.VMEM(t.shape, t.dtype) for t in sources.values()),
        in_specs=[anywhere] * (1 + len(sources)),
        out_specs=(anywhere,) + (here,) * len(sources),
        scratch_shapes=pack_scratch
        + [pltpu.SemaphoreType.DMA((len(sources),)), chunk_sems, chunk_sems],
        cost_estimate=pl.CostEstimate(flops=5_000_000_000, bytes_accessed=1024, transcendentals=0),
        compiler_params=pltpu.CompilerParams(vmem_limit_bytes=58 * 1024 * 1024),
    )(spectral_weight, *sources.values())
    held = dict(zip(sources, held))
    a_part = call(
        first_kernel,
        rows_of(plan.mx + EDGE),
        field_c,
        use=("col", "row") + edge_tables,
        mib=20,
    )
    a_both = exchange(a_part)
    weights = call(
        lambda plan, held, r_ref, after_ref, first_ref, *refs: pack_rows(
            plan, early, late, r_ref, *refs
        ),
        jax.ShapeDtypeStruct(packed_shape, BF16),
        raw=(spectral_weight, a_part, weights),
        scratch=pack_scratch + [chunk_sems, chunk_sems],
        spec=anywhere,
        us=5.0,
        alias=True,
    )
    b_part, a_kept = call(
        mix_kernel,
        (rows_of(plan.mx + 2 * plan.rows), rows_of(plan.mx)),
        a_both,
        raw=(weights, field, cotangent.reshape(n, plan.rows, by), kernel_weight),
        scratch=[place, kernel_place, pltpu.SemaphoreType.DMA((2,))]
        + [block, edges, paired, taps]
        + modes_scratch
        + [pltpu.SemaphoreType.DMA],
        us=6.0,
        mib=54,
    )
    g_part = call(
        middle_kernel,
        rows_of(plan.mx + plan.rows + EDGE),
        exchange(b_part),
        use=("row_s", "col", "row") + edge_tables,
        mib=20,
        scratch=[pltpu.VMEM((plan.nx, cpd * plan.ny), BF16)],
        us=2.6,
    )
    g_both = exchange(g_part)
    layer_out, grad_sum, back_terms, g_kept = call(
        back_kernel,
        (
            jax.ShapeDtypeStruct(field.shape, BF16),
            jax.ShapeDtypeStruct(field.shape, F32),
            rows_of(plan.mx + EDGE),
            rows_of(plan.mx),
        ),
        g_both,
        raw=(weights, field, cotangent, kernel_weight),
        scratch=[place, place, kernel_place, pltpu.SemaphoreType.DMA((3,))]
        + [block, edges, paired, taps, field_flat]
        + modes_scratch,
        us=8.0,
        mib=54,
    )
    back_both = exchange(back_terms)

    def outer_part(first_j, count, after, alias):
        return call(
            lambda plan, *refs: outer_kernel(plan, first_j, count, *refs),
            jax.ShapeDtypeStruct(spectral_weight.shape, BF16),
            a_kept,
            g_kept,
            scratch=[
                flat,
                flat,
                turned,
                turned,
                pltpu.VMEM((2, count, plan.my, channels, channels), BF16),
                pltpu.SemaphoreType.DMA((count // CHUNK,)),
            ],
            spec=anywhere,
            us=6.4,
            after=after,
            alias=alias,
        )

    spectral_half = outer_part(0, half, (back_terms,), False)
    last_part = call(
        last_kernel,
        rows_of(plan.rows + EDGE),
        back_both,
        use=("row_s", "col"),
        us=1.3,
        mib=44,
        after=(spectral_half,),
    )
    last_both = exchange(last_part)
    spectral_grad = outer_part(half, half, (last_part, spectral_half), True)
    field_grad, kernel_grad = call(
        end_kernel,
        (
            jax.ShapeDtypeStruct(field.shape, BF16),
            jax.ShapeDtypeStruct((3, 3, channels, channels), F32),
        ),
        last_both,
        grad_sum,
        scratch=[edges],
        mib=20,
    )
    return (layer_out, field_grad, spectral_grad, kernel_grad)


def body(field, spectral_weight, kernel_weight, cotangent):
    plan = Plan(*field.shape, lax.axis_size("gx"), lax.axis_size("gy"))
    if plan.fits:
        return fast_body(plan, field, spectral_weight, kernel_weight, cotangent)
    return general_body(field, spectral_weight, kernel_weight, cotangent)


def solution(mesh):
    in_specs = (P(None, "gx", "gy"), P(None, "gx", "gy", None, None), P(), P(None, "gx", "gy"))
    out_specs = (P(None, "gx", "gy"), P(None, "gx", "gy"), P(None, "gx", "gy", None, None), P())
    return jax.shard_map(body, mesh=mesh, in_specs=in_specs, out_specs=out_specs, check_vma=False)
```
